512 devices in a mesh: seq: 32 (over x, y, core), exp: 16 (over z).
Axes of the slice: x: 4, y: 4, z: 16, core: 2. Of those that a mesh axis runs over, the one named last changes fastest.
Arguments:
- tokens: bfloat16 [65536, 1024], P('seq', 'exp'), may hold values from -12 to 12
- routing: bfloat16 [1024, 2048], P(None, 'exp'), may hold values from -2 to 2
- w_in: bfloat16 [128, 1024, 4096], P('exp', None, 'seq'), may hold values from -0.1875 to 0.1875
- w_out: bfloat16 [128, 4096, 1024], P('exp', 'seq'), may hold values from -0.09375 to 0.09375
Outputs:
- mixed_tokens: bfloat16 [65536, 1024], P('seq', 'exp')
The draws below stay inside these ranges and needn't reach their ends.
All inputs are finite; a program needn't handle non-finite values.
Results may differ from the reference program's by a relative error of at most 0.02.
Values may be sent and summed in bfloat16 or wider, within the bound.
A program may use at most 128 MiB of HBM per device.

```python
import math
import jax
import jax.numpy as jnp
from jax import lax

D = 1024
FF = 4096
SLOTS_PER = 16
EXP_DEV = 8
TOK_DEV = 2048
EXPERTS = 128
SLOTS = 2048
TOKENS = 65536
N_SEQ = 32
N_EXP = 16


reach_level = 2.5


reach_logit = 32.0


reach_gap = 6.8


spread_level = 0.15


def plant_layout(key):
    block_count = TOKENS // TOK_DEV
    group_width = EXP_DEV * SLOTS_PER
    group_count = SLOTS // group_width
    first_block = jax.random.randint(jax.random.fold_in(key, 201), (), 0, block_count, dtype=jnp.int32)
    second_block = (first_block + 1 + jax.random.randint(jax.random.fold_in(key, 202), (), 0, block_count - 1, dtype=jnp.int32)) % block_count
    first_rows = first_block * TOK_DEV + jax.random.permutation(jax.random.fold_in(key, 203), TOK_DEV).astype(jnp.int32)
    second_rows = second_block * TOK_DEV + jax.random.permutation(jax.random.fold_in(key, 204), TOK_DEV).astype(jnp.int32)
    group_order = jax.random.permutation(jax.random.fold_in(key, 205), group_count).astype(jnp.int32)
    slot_offsets = jax.random.permutation(jax.random.fold_in(key, 206), group_width).astype(jnp.int32)
    reach_count = min(TOK_DEV - 3, 8)
    reach_rows = jnp.concatenate([first_rows[3:3 + reach_count], second_rows[3:3 + reach_count]])
    flat_start = (group_order[0] * group_width).astype(jnp.int32)
    peak_slot = group_order[1] * group_width + slot_offsets[0]
    return (reach_rows, flat_start, peak_slot)


def reach_pattern(key):
    reach_count = min(TOK_DEV - 3, 8)
    signs = jnp.where(jax.random.bernoulli(jax.random.fold_in(key, 211), 0.5, (D,)), 1.0, -1.0).astype(jnp.float32)
    column_mags = jax.random.uniform(jax.random.fold_in(key, 212), (D,), jnp.float32, 0.5, 1.5)
    row_mags = jax.random.uniform(jax.random.fold_in(key, 213), (2 * reach_count, D), jnp.float32, 0.5, 1.5)
    return (signs * column_mags, reach_level * signs[None, :] * row_mags)


def draw_tokens(key, part):
    reach_rows, flat_start, peak_slot = plant_layout(key)
    reach_column, reach_tokens = reach_pattern(key)
    key = jax.random.fold_in(key, 1)
    key_base, key_scale = jax.random.split(key, 2)
    row_scale = jnp.exp(jax.random.uniform(key_scale, (TOKENS, 1), jnp.float32, math.log(0.3), math.log(3.0)))
    base_draw = jax.random.truncated_normal(key_base, -4.0, 4.0, (TOKENS, D), jnp.float32)
    matrix = base_draw * row_scale
    matrix = matrix.at[reach_rows].set(reach_tokens)
    return matrix.astype(jnp.bfloat16)


def draw_routing(key, part):
    reach_rows, flat_start, peak_slot = plant_layout(key)
    reach_column, reach_tokens = reach_pattern(key)
    key = jax.random.fold_in(key, 2)
    key_base, key_scale, key_spread, key_peak = jax.random.split(key, 4)
    column_scale = jnp.exp(jax.random.uniform(key_scale, (1, SLOTS), jnp.float32, math.log(0.5), math.log(2.5)))
    base_draw = jax.random.truncated_normal(key_base, -4.0, 4.0, (D, SLOTS), jnp.float32) * D ** (-0.5)
    matrix = base_draw * column_scale
    group_width = EXP_DEV * SLOTS_PER
    reach_scale = reach_logit / (reach_level * D)
    spread_noise = jax.random.uniform(key_spread, (D, group_width), jnp.float32, -1.0, 1.0)
    flat_block = (reach_scale * reach_column[:, None] * (1.0 + spread_level * spread_noise)).astype(matrix.dtype)
    matrix = lax.dynamic_update_slice(matrix, flat_block, (jnp.zeros((), jnp.int32), flat_start))
    peak_noise = jax.random.uniform(key_peak, (D,), jnp.float32, -1.0, 1.0)
    peak_column = (1.0 + reach_gap / reach_logit) * reach_scale * reach_column * (1.0 + spread_level * peak_noise)
    matrix = matrix.at[:, peak_slot].set(peak_column)
    return matrix.astype(jnp.bfloat16)


def block_levels(rng, shape, pieces, least, high):
    level = 1.0
    for dim, shards_of in pieces:
        steps = jax.random.uniform(jax.random.fold_in(jax.random.fold_in(rng, 6), dim), (shards_of,), jnp.float32, least / len(pieces), high / len(pieces))
        level = level * jnp.repeat(jnp.exp(steps), shape[dim] // shards_of).reshape((-1,) + (1,) * (len(shape) - 1 - dim))
    return level


def normal_values(stream_key, shape, width, bound, shards=(), held_as=jnp.bfloat16):
    drawn = width * jax.random.normal(stream_key, shape, jnp.float32)
    if shards:
        drawn = drawn * block_levels(stream_key, shape, shards, -0.22, 0.18)
    return jnp.clip(drawn, -bound, bound).astype(held_as)


def setup_inputs(seed: int = 0) -> dict:
    splits = jax.random.split(jax.random.key(seed), 5)
    tokens = draw_tokens(jax.random.fold_in(splits[4], 71), 0)
    routing = draw_routing(jax.random.fold_in(splits[4], 71), 0)
    w_in = normal_values(splits[2], (EXPERTS, D, FF), D ** -0.5, 0.1875, ((0, 16), (2, 32)))
    w_out = normal_values(splits[3], (EXPERTS, FF, D), FF ** -0.5, 0.09375, ((0, 16), (1, 32)))
    return dict(tokens=tokens, routing=routing, w_in=w_in, w_out=w_out)


def block_stats(token_block, routing):
    logits = jnp.dot(token_block, routing, preferred_element_type=jnp.float32)
    local_peak = jnp.max(logits, axis=0)
    exponent = jnp.exp(logits - local_peak)
    local_total = jnp.sum(exponent, axis=0)
    local_rows = lax.dot_general(exponent.astype(jnp.bfloat16), token_block, (((0,), (0,)), ((), ())), preferred_element_type=jnp.float32)
    return local_peak, local_total, local_rows


def expert_step(operands):
    slot_block, inner_weight, outer_weight = operands
    hidden = jax.nn.gelu(jnp.dot(slot_block, inner_weight, preferred_element_type=jnp.float32), approximate=True).astype(jnp.bfloat16)
    return jnp.dot(hidden, outer_weight, preferred_element_type=jnp.float32).astype(jnp.bfloat16)


def reference(tokens, routing, w_in, w_out):
    blocks = tokens.reshape(N_SEQ, TOK_DEV, D)
    peaks, totals, rows_all = lax.map(lambda token_block: block_stats(token_block, routing), blocks)
    slot_peak = jnp.max(peaks, axis=0)
    scales = jnp.exp(peaks - slot_peak)
    numerator = jnp.sum(rows_all * scales[:, :, None], axis=0)
    denominator = jnp.sum(totals * scales, axis=0)
    slot_inputs = (numerator / denominator[:, None]).astype(jnp.bfloat16)
    grouped = slot_inputs.reshape(EXPERTS, SLOTS_PER, D)
    expert_out = lax.map(expert_step, (grouped, w_in, w_out)).reshape(SLOTS, D)
    expert_groups = expert_out.reshape(N_EXP, EXP_DEV * SLOTS_PER, D).astype(jnp.float32)

    def combine(token_block):
        logits = jnp.dot(token_block, routing, preferred_element_type=jnp.float32)
        token_peak = jnp.max(logits, axis=1, keepdims=True)
        exponent = jnp.exp(logits - token_peak)
        token_total = jnp.sum(exponent, axis=1)
        weight_blocks = exponent.astype(jnp.bfloat16).astype(jnp.float32).reshape(TOK_DEV, N_EXP, EXP_DEV * SLOTS_PER)
        group_rows = jnp.einsum("tgs,gsd->gtd", weight_blocks, expert_groups).astype(jnp.bfloat16)
        summed = jnp.sum(group_rows.astype(jnp.float32), axis=0)
        return (summed / token_total[:, None]).astype(jnp.bfloat16)

    return lax.map(combine, blocks).reshape(TOKENS, D)
```

```python
import functools

import jax
import jax.numpy as jnp
from jax import lax
from jax.experimental import pallas as pl
from jax.experimental.pallas import tpu as pltpu
from jax.sharding import PartitionSpec as P

MESH = pl.DeviceIdType.MESH
F32, BF16 = jnp.float32, jnp.bfloat16
N = 4
CHIPS = N * N
ROWS = 64
HALF = ROWS // 2
TOK = 128
FSET = {1: (2, 1), -1: (-1, 0)}


def remote(src, dst, send, recv, seq, z):
    return pltpu.make_async_remote_copy(
        src_ref=src, dst_ref=dst, send_sem=send, recv_sem=recv, device_id=(seq, z), device_id_type=MESH
    )


def kernel(nz, tok_ref, route_ref, win_ref, wout_ref, out_ref, *scratch):
    (
        xt, gr, ge, lg, wt, cw, stok, s, rf, rn, rf2, rn2, fb, mx, mxr, tt, ttr, zs, zst, zb, si, sp, pacc,
        pt, pb, osend, orecv, oown, ofin, trow, trow_r, prow, win, wout,
        tok_s, tok_r, xs_s, xs_r, rz_s, rz_r, ag_s, ag_r, ae_s, ae_r, rs_s, rs_r, mx_s, mx_r, tt_s, tt_r, zs_s, zs_r,
        zb_s, zb_r, si_s, si_r, pt_s, pt_r, ez_s, ez_r, os_s, os_r, fin_s, fin_r, tr_s, tr_r, w_s, own_s,
    ) = scratch
    seq, z = lax.axis_index("seq"), lax.axis_index("exp")
    x, y, c = seq // (2 * N), (seq // 2) % N, seq % 2
    p = seq // 2
    planes = nz // 2
    width = 128 * planes
    feats = xt.shape[0]
    fz = feats // nz
    owner = c == z % 2
    oc = z % 2
    mine = pl.multiple_of((z // 2) * 128, 128)
    other = 2 * p + 1 - c

    def zpeer(k):
        return (z + k) % nz

    def chip(k):
        return (p + k) % CHIPS

    def lanes(j):
        return pl.ds(pl.multiple_of(j * 128, 128), 128)

    def rows(i, n):
        return pl.ds(pl.multiple_of(i * n, n), n)

    def loop(lo, hi):
        def run(body):
            def step(i, carry):
                body(i)
                return carry
            lax.fori_loop(lo, hi, step, 0)
        return run

    barrier = pltpu.get_barrier_semaphore()

    @loop(1, nz)
    def _(k):
        pl.semaphore_signal(barrier, inc=1, device_id=(seq, zpeer(k)), device_id_type=MESH)

    @loop(1, CHIPS)
    def _(k):
        pl.semaphore_signal(barrier, inc=1, device_id=(2 * chip(k) + c, z), device_id_type=MESH)
        pl.semaphore_signal(barrier, inc=1, device_id=(2 * chip(k) + 1 - c, z), device_id_type=MESH)

    pl.semaphore_signal(barrier, inc=1, device_id=(other, z), device_id_type=MESH)

    own_x = pltpu.make_async_copy(tok_ref.at[:, lanes(z)], xt.at[rows(z, fz), lanes(c)], own_s.at[0])
    own_x.start()
    own_r = pltpu.make_async_copy(route_ref.at[rows(p, ROWS), :], gr.at[x, y, :, pl.ds(mine, 128)], own_s.at[1])

    @pl.when(owner)
    def _():
        own_r.start()

    load_in = pltpu.make_async_copy(win_ref, win, w_s.at[0])
    load_out = pltpu.make_async_copy(wout_ref, wout, w_s.at[1])

    pl.semaphore_wait(barrier, nz - 1 + 2 * (CHIPS - 1) + 1)

    def rz_copy(k):
        return remote(
            route_ref.at[rows(p, ROWS), :], gr.at[x, y, :, pl.ds(mine, 128)], rz_s.at[k], rz_r.at[z // 2], seq, zpeer(k)
        )

    @pl.when(owner)
    def _():
        @loop(1, nz)
        def _(k):
            rz_copy(k).start()

    def tok_copy(k):
        to = zpeer(k)
        return remote(
            tok_ref.at[:, lanes(to)], xt.at[rows(z, fz), lanes(c)], tok_s.at[k], tok_r.at[z], seq, to
        )

    @loop(1, nz)
    def _(k):
        tok_copy(k).start()

    load_in.start()
    load_out.start()

    def near(h, axis, d):
        along_x = (axis == 1) == (h == 0)
        nx = (x + d) % N if along_x else x
        ny = y if along_x else (y + d) % N
        return 2 * (N * nx + ny) + c

    def place(h, o1, o2):
        return ((x + o1) % N, (y + o2) % N) if h == 0 else ((x + o2) % N, (y + o1) % N)

    def block(buf, h, o1, o2, lo=0, n=HALF):
        bx, by = place(h, o1, o2)
        return buf.at[bx, by, pl.ds(h * HALF + lo, n), :]

    OFF = (0, 1, -1, 2)
    QUART = HALF // 2

    def gather(buf, ss, rs):
        def s1(h, d):
            b = block(buf, h, 0, 0)
            i = 16 * h + (0 if d == 1 else 1)
            return remote(b, b, ss.at[i], rs.at[i], near(h, 1, d), z)

        def s1f(h, d):
            b = block(buf, h, -d, 0, 0 if d == 1 else QUART, QUART)
            i = 16 * h + (2 if d == 1 else 3)
            return remote(b, b, ss.at[i], rs.at[i], near(h, 1, d), z)

        def s2(h, d, o):
            b = block(buf, h, o, 0)
            i = 16 * h + 4 + 4 * (d == -1) + OFF.index(o)
            return remote(b, b, ss.at[i], rs.at[i], near(h, 2, d), z)

        def s2f(h, d, o):
            b = block(buf, h, o, -d)
            i = 16 * h + 12 + 2 * (d == -1) + FSET[d].index(o)
            return remote(b, b, ss.at[i], rs.at[i], near(h, 2, d), z)

        both = (0, 1)
        dirs = (1, -1)
        sent = []

        def go(copy):
            copy.start()
            sent.append(copy)

        def got1(h, d):
            b = block(buf, h, -d, 0)
            i = 16 * h + (0 if d == 1 else 1)
            remote(b, b, ss.at[i], rs.at[i], near(h, 1, d), z).wait_recv()

        def got1f(h, d):
            b = block(buf, h, 2, 0, 0 if d == 1 else QUART, QUART)
            i = 16 * h + (2 if d == 1 else 3)
            remote(b, b, ss.at[i], rs.at[i], near(h, 1, d), z).wait_recv()

        def got2(h, d, o):
            b = block(buf, h, o, -d)
            i = 16 * h + 4 + 4 * (d == -1) + OFF.index(o)
            remote(b, b, ss.at[i], rs.at[i], near(h, 2, d), z).wait_recv()

        def got2f(h, d, o):
            b = block(buf, h, o, 2)
            i = 16 * h + 12 + 2 * (d == -1) + FSET[d].index(o)
            remote(b, b, ss.at[i], rs.at[i], near(h, 2, d), z).wait_recv()

        for h in both:
            for d in dirs:
                go(s1(h, d))
        for h in both:
            for d in dirs:
                go(s2(h, d, 0))
        for d in dirs:
            for h in both:
                got1(h, d)
                go(s1f(h, d))
                go(s2(h, 1, -d))
                go(s2(h, -1, -d))
        for h in both:
            got2(h, -1, 0)
            go(s2f(h, -1, 0))
        for h in both:
            for d in dirs:
                got1f(h, d)
            for d in dirs:
                go(s2(h, d, 2))
        for h in both:
            got2(h, 1, 1)
            go(s2f(h, 1, 1))
            got2(h, -1, -1)
            go(s2f(h, -1, -1))
        for h in both:
            got2(h, 1, 2)
            go(s2f(h, 1, 2))
        for h in both:
            for d, o in ((1, 0), (1, -1), (-1, 1), (-1, 2)):
                got2(h, d, o)
            for d in dirs:
                for o in FSET[d]:
                    got2f(h, d, o)
        return sent

    def scatter(buf, ss, rs):
        both = (0, 1)
        dirs = (1, -1)
        sent = []

        def go(copy):
            copy.start()
            sent.append(copy)

        def slot_f(h, d, o):
            return 4 * h + 2 * (d == -1) + FSET[d].index(o)

        def slot_n(h, d, o):
            return 8 * h + 4 * (d == -1) + OFF.index(o)

        def slot_2(h, d):
            return 2 * h + (d == -1)

        def r1f(h, d, o):
            i = slot_f(h, d, o)
            return remote(block(buf, h, o, 2), rf.at[i], ss.at[i], rs.at[i], near(h, 2, d), z)

        def r1(h, d, o):
            i = slot_n(h, d, o)
            return remote(block(buf, h, o, d), rn.at[i], ss.at[8 + i], rs.at[8 + i], near(h, 2, d), z)

        def r2f(h, d):
            i = slot_2(h, d)
            b = block(buf, h, 2, 0, 0 if d == 1 else QUART, QUART)
            return remote(b, rf2.at[i], ss.at[24 + i], rs.at[24 + i], near(h, 1, d), z)

        def r2(h, d):
            i = slot_2(h, d)
            return remote(block(buf, h, d, 0), rn2.at[i], ss.at[28 + i], rs.at[28 + i], near(h, 1, d), z)

        for d, n in ((1, 0), (-1, 0), (1, 1), (-1, 1)):
            for h in both:
                go(r1f(h, d, FSET[d][n]))
        for h in both:
            go(r1(h, -1, 2))
            go(r1(h, 1, -1))
        for h in both:
            go(r1(h, -1, 1))
            go(r1(h, 1, 0))
        for d, n in ((1, 0), (-1, 0), (1, 1), (-1, 1)):
            for h in both:
                o = FSET[d][n]
                r1f(h, d, o).wait_recv()
                b = block(buf, h, o, d)
                b[...] = (b[...].astype(F32) + rf[slot_f(h, d, o)].astype(F32)).astype(BF16)
                go(r1(h, d, o))

        def total(h, o):
            r1(h, 1, o).wait_recv()
            r1(h, -1, o).wait_recv()
            b = block(buf, h, o, 0)
            return b[...].astype(F32) + rn[slot_n(h, 1, o)].astype(F32) + rn[slot_n(h, -1, o)].astype(F32)

        for h in both:
            block(buf, h, 2, 0)[...] = total(h, 2).astype(BF16)
            go(r2f(h, 1))
            go(r2f(h, -1))
        for h in both:
            for d in dirs:
                block(buf, h, d, 0)[...] = total(h, d).astype(BF16)
        for h in both:
            for d in dirs:
                r2f(h, d).wait_recv()
                b = block(buf, h, d, 0, 0 if d == 1 else QUART, QUART)
                b[...] = (b[...].astype(F32) + rf2[slot_2(h, d)].astype(F32)).astype(BF16)
                go(r2(h, d))
        for h in both:
            mid = total(h, 0)
            r2(h, 1).wait_recv()
            r2(h, -1).wait_recv()
            fb[pl.ds(h * HALF, HALF), :] = (
                mid + rn2[slot_2(h, 1)].astype(F32) + rn2[slot_2(h, -1)].astype(F32)
            ).astype(BF16)
        return sent

    def from_planes(copy_of):
        @loop(0, planes)
        def _(j):
            @pl.when(2 * j + c != z)
            def _():
                copy_of(j).wait_recv()

    def rz_got(j):
        return remote(
            route_ref.at[rows(p, ROWS), :], gr.at[x, y, :, lanes(j)], rz_s.at[0], rz_r.at[j], seq, z
        )

    from_planes(rz_got)

    @pl.when(owner)
    def _():
        own_r.wait()

    sent_r = gather(gr, ag_s, ag_r)

    own_x.wait()
    groups = min(4, nz)
    per = nz // groups
    depth = feats // groups

    def xs_copy(g, half):
        b = xt.at[pl.ds(g * depth, depth), lanes(half)]
        return remote(b, b, xs_s.at[g], xs_r.at[g], other, z)

    for g in range(groups):
        for i in range(per):
            frm = g * per + i

            @pl.when(frm != z)
            def _():
                remote(
                    tok_ref.at[:, lanes(z)], xt.at[pl.ds(frm * fz, fz), lanes(c)], tok_s.at[0], tok_r.at[frm], seq, z
                ).wait_recv()

        xs_copy(g, c).start()
    for g in range(groups):
        xs_copy(g, 1 - c).wait_recv()

    stok[...] = xt[...].T
    tile = min(256, width)

    @loop(0, width // tile)
    def _(j):
        at = pl.ds(pl.multiple_of(j * tile, tile), tile)
        part = gr[:, :, :, at].reshape(feats, tile)
        val = jnp.dot(stok[...], part, preferred_element_type=F32)
        lg[:, at] = val
        mrow = jnp.max(val, axis=0, keepdims=True)
        for t in range(tile // 128):
            mx[pl.ds(j * (tile // 128) + t, 1), :] = mrow[:, 128 * t : 128 * (t + 1)]

    if planes < 8:
        mx[planes:8, :] = jnp.zeros((8 - planes, 128), F32)

    def mx_copy(src, dst, ss, rs, k):
        return remote(src, dst.at[p], ss.at[k], rs.at[p], 2 * chip(k) + c, z)

    @loop(1, CHIPS)
    def _(k):
        mx_copy(mx, mxr, mx_s, mx_r, k).start()

    peak = jnp.max(lg[...], axis=1, keepdims=True)
    expo = jnp.exp(lg[...] - peak)
    cw[...] = expo.astype(BF16)
    tsum = jnp.sum(expo, axis=1, keepdims=True)
    peak_t = jnp.broadcast_to(peak, (2 * TOK, 128)).T
    tsum_t = jnp.broadcast_to(tsum, (2 * TOK, 128)).T
    trow[0:8, :] = peak_t[0:8, :]
    trow[8:16, :] = tsum_t[0:8, :]
    tr_copy = remote(trow, trow_r, tr_s.at[0], tr_r.at[0], other, z)
    tr_copy.start()

    def from_chips(dst, ss, rs):
        @loop(1, CHIPS)
        def _(k):
            remote(mx, dst.at[chip(k)], ss.at[0], rs.at[chip(k)], seq, z).wait_recv()

    mxr[p] = mx[...]
    from_chips(mxr, mx_s, mx_r)
    plane_peak = jnp.max(mxr[...], axis=0)
    for j in range(planes):
        prow[:, 128 * j : 128 * (j + 1)] = plane_peak[j : j + 1, :]

    expo = jnp.exp(lg[...] - prow[...])
    wt[...] = expo.astype(BF16)
    ssum = jnp.sum(expo, axis=0, keepdims=True)
    for j in range(planes):
        tt[j : j + 1, :] = ssum[:, 128 * j : 128 * (j + 1)]
    if planes < 8:
        tt[planes:8, :] = jnp.zeros((8 - planes, 128), F32)

    @loop(1, CHIPS)
    def _(k):
        mx_copy(tt, ttr, tt_s, tt_r, k).start()

    @loop(0, N)
    def _(i):
        part = xt[rows(i, feats // N), :]
        s[i] = jnp.dot(part, wt[...], preferred_element_type=F32).astype(BF16).reshape(N, ROWS, width)

    ttr[p] = tt[...]
    from_chips(ttr, tt_s, tt_r)
    plane_sum = jnp.sum(ttr[...], axis=0)
    for j in range(planes):
        zs[j, 0:1, :] = plane_peak[j : j + 1, :]
        zs[j, 1:2, :] = plane_sum[j : j + 1, :]
        zs[j, 2:8, :] = jnp.zeros((6, 128), F32)

    def zs_copy(j):
        return remote(zs.at[j], zst.at[z], zs_s.at[j], zs_r.at[z], seq, 2 * j + c)

    def to_planes(do):
        @loop(0, planes)
        def _(j):
            @pl.when(2 * j + c != z)
            def _():
                do(j)

    to_planes(lambda j: zs_copy(j).start())

    sent_s = scatter(s, rs_s, rs_r)

    def zb_copy(j):
        return remote(fb.at[:, lanes(j)], zb.at[z], zb_s.at[j], zb_r.at[z], seq, 2 * j + c)

    to_planes(lambda j: zb_copy(j).start())

    def si_copy(k, core, sem):
        return remote(si.at[p], si.at[p], sem, si_r.at[p], 2 * chip(k) + core, z)

    @pl.when(owner)
    def _():
        zst[z] = zs[z // 2]
        zb[z] = fb[:, pl.ds(mine, 128)]

        @loop(1, nz)
        def _(k):
            frm = zpeer(k)
            remote(zs.at[0], zst.at[frm], zs_s.at[0], zs_r.at[frm], seq, z).wait_recv()

        stat = zst[...]
        peaks = stat[:, 0:1, :]
        scale = jnp.exp(peaks - jnp.max(peaks, axis=0, keepdims=True))
        below = jnp.sum(scale * stat[:, 1:2, :], axis=0)

        @loop(1, nz)
        def _(k):
            frm = zpeer(k)
            remote(fb.at[:, lanes(0)], zb.at[frm], zb_s.at[0], zb_r.at[frm], seq, z).wait_recv()

        above = jnp.sum(scale * zb[...].astype(F32), axis=0)
        si[p] = (above / below).astype(BF16)

        @loop(1, CHIPS)
        def _(k):
            si_copy(k, c, si_s.at[k]).start()
            si_copy(k, 1 - c, si_s.at[CHIPS + k]).start()

        si_copy(0, 1 - c, si_s.at[CHIPS]).start()

    load_in.wait()
    load_out.wait()

    @loop(1, CHIPS)
    def _(k):
        remote(si.at[p], si.at[chip(k)], si_s.at[0], si_r.at[chip(k)], seq, z).wait_recv()

    @pl.when(jnp.logical_not(owner))
    def _():
        remote(si.at[p], si.at[p], si_s.at[0], si_r.at[p], seq, z).wait_recv()

    sp[...] = si[...].reshape(feats, 128).T
    experts = win.shape[0]
    each = 128 // experts

    @loop(0, experts)
    def _(e):
        h = jnp.dot(sp[rows(e, each), :], win[e], preferred_element_type=F32)
        h = jax.nn.gelu(h, approximate=True).astype(BF16)
        pacc[rows(e, each), :] = jnp.dot(h, wout[e], preferred_element_type=F32)

    pt[...] = pacc[...].T.astype(BF16).reshape(CHIPS, ROWS, 128)

    def pt_copy(k):
        return remote(pt.at[chip(k)], pb.at[seq], pt_s.at[k], pt_r.at[seq], 2 * chip(k) + oc, z)

    @loop(1, CHIPS)
    def _(k):
        pt_copy(k).start()

    @pl.when(jnp.logical_not(owner))
    def _():
        pt_copy(0).start()

    def ez_copy(k):
        b = ge.at[x, y, :, pl.ds(mine, 128)]
        return remote(b, b, ez_s.at[k], ez_r.at[z // 2], seq, zpeer(k))

    @pl.when(owner)
    def _():
        pb[seq] = pt[p]

        @loop(1, 2 * CHIPS)
        def _(k):
            frm = (seq + k) % (2 * CHIPS)
            remote(pt.at[0], pb.at[frm], pt_s.at[0], pt_r.at[frm], seq, z).wait_recv()

        ge[x, y, :, pl.ds(mine, 128)] = jnp.sum(pb[...].astype(F32), axis=0).astype(BF16)

        @loop(1, nz)
        def _(k):
            ez_copy(k).start()

    def ez_got(j):
        b = ge.at[x, y, :, lanes(j)]
        return remote(b, b, ez_s.at[0], ez_r.at[j], seq, z)

    from_planes(ez_got)
    sent_e = gather(ge, ae_s, ae_r)

    tr_copy.wait_recv()
    my = pl.multiple_of(c * TOK, TOK)
    their = pl.multiple_of((1 - c) * TOK, TOK)
    peak_a, peak_b = trow[0:1, pl.ds(my, TOK)], trow_r[0:1, pl.ds(my, TOK)]
    sum_a, sum_b = trow[8:9, pl.ds(my, TOK)], trow_r[8:9, pl.ds(my, TOK)]
    top = jnp.maximum(peak_a, peak_b)
    fac_a, fac_b = jnp.exp(peak_a - top), jnp.exp(peak_b - top)
    under = fac_a * sum_a + fac_b * sum_b
    fac_a, fac_b = fac_a / under, fac_b / under

    def os_copy(g):
        return remote(osend.at[g], orecv.at[g], os_s.at[g], os_r.at[g], other, z)

    def fin_copy(g, i):
        to = g * per + i
        return remote(ofin.at[to], out_ref.at[:, lanes(z)], fin_s.at[to], fin_r.at[z], seq, to)

    blocks = N // groups

    @loop(0, groups)
    def _(g):
        part = ge[pl.ds(g * blocks, blocks)].reshape(depth, width)
        both = lax.dot_general(part, cw[...], (((1,), (1,)), ((), ())), preferred_element_type=F32)
        first, second = both[:, :TOK], both[:, TOK:]
        oown[g] = jnp.where(c == 0, first, second)
        osend[g] = jnp.where(c == 0, second, first).astype(BF16)
        os_copy(g).start()

    own_o = pltpu.make_async_copy(ofin.at[z], out_ref.at[:, lanes(z)], own_s.at[2])

    @loop(0, groups)
    def _(g):
        os_copy(g).wait_recv()
        val = (oown[g] * fac_a + orecv[g].astype(F32) * fac_b).astype(BF16).reshape(per, fz, TOK)

        for i in range(per):
            to = g * per + i
            ofin[to] = val[i]

            @pl.when(to != z)
            def _():
                fin_copy(g, i).start()

            @pl.when(to == z)
            def _():
                own_o.start()

    own_o.wait()

    @loop(1, nz)
    def _(k):
        to = zpeer(k)
        remote(ofin.at[to], out_ref.at[:, lanes(to)], fin_s.at[to], fin_r.at[to], seq, z).wait()

    @loop(1, nz)
    def _(k):
        tok_copy(k).wait_send()

    @pl.when(owner)
    def _():
        @loop(1, nz)
        def _(k):
            rz_copy(k).wait_send()
            ez_copy(k).wait_send()

        @loop(1, CHIPS)
        def _(k):
            si_copy(k, c, si_s.at[k]).wait_send()
            si_copy(k, 1 - c, si_s.at[CHIPS + k]).wait_send()

        si_copy(0, 1 - c, si_s.at[CHIPS]).wait_send()

    @loop(1, CHIPS)
    def _(k):
        mx_copy(mx, mxr, mx_s, mx_r, k).wait_send()
        mx_copy(tt, ttr, tt_s, tt_r, k).wait_send()
        pt_copy(k).wait_send()

    @pl.when(jnp.logical_not(owner))
    def _():
        pt_copy(0).wait_send()

    to_planes(lambda j: zs_copy(j).wait_send())
    to_planes(lambda j: zb_copy(j).wait_send())
    tr_copy.wait_send()
    for g in range(groups):
        xs_copy(g, c).wait_send()
        os_copy(g).wait_send()
    for copy in sent_r + sent_s + sent_e:
        copy.wait_send()


def shards(nz, tokens, routing, w_in, w_out):
    tokens_t = tokens.T
    fz = tokens_t.shape[0]
    feats = fz * nz
    planes = nz // 2
    width = 128 * planes
    groups = min(4, nz)
    depth = feats // groups
    v, dma = pltpu.VMEM, pltpu.SemaphoreType.DMA
    scratch = [
        v((feats, 2 * TOK), BF16),
        v((N, N, ROWS, width), BF16),
        v((N, N, ROWS, width), BF16),
        v((2 * TOK, width), F32),
        v((2 * TOK, width), BF16),
        v((2 * TOK, width), BF16),
        v((2 * TOK, feats), BF16),
        v((N, N, ROWS, width), BF16),
        v((8, HALF, width), BF16),
        v((16, HALF, width), BF16),
        v((4, HALF // 2, width), BF16),
        v((4, HALF, width), BF16),
        v((ROWS, width), BF16),
        v((8, 128), F32),
        v((CHIPS, 8, 128), F32),
        v((8, 128), F32),
        v((CHIPS, 8, 128), F32),
        v((planes, 8, 128), F32),
        v((nz, 8, 128), F32),
        v((nz, ROWS, 128), BF16),
        v((CHIPS, ROWS, 128), BF16),
        v((128, feats), BF16),
        v((128, feats), F32),
        v((CHIPS, ROWS, 128), BF16),
        v((2 * CHIPS, ROWS, 128), BF16),
        v((groups, depth, TOK), BF16),
        v((groups, depth, TOK), BF16),
        v((groups, depth, TOK), F32),
        v((nz, fz, TOK), BF16),
        v((16, 2 * TOK), F32),
        v((16, 2 * TOK), F32),
        v((1, width), F32),
        v(w_in.shape, BF16),
        v(w_out.shape, BF16),
    ]
    counts = [
        nz, nz, groups, groups, nz, planes, 32, 32, 32, 32, 32, 32, CHIPS, CHIPS, CHIPS, CHIPS, planes, nz,
        planes, nz, 2 * CHIPS, CHIPS, CHIPS, 2 * CHIPS, nz, planes, groups, groups, nz, nz, 1, 1, 2, 3,
    ]
    scratch += [dma((n,)) for n in counts]
    out = pl.pallas_call(
        functools.partial(kernel, nz),
        out_shape=jax.ShapeDtypeStruct(tokens_t.shape, BF16),
        in_specs=[pl.BlockSpec(memory_space=pl.ANY)] * 4,
        out_specs=pl.BlockSpec(memory_space=pl.ANY),
        scratch_shapes=scratch,
        compiler_params=pltpu.CompilerParams(
            collective_id=0, has_side_effects=True, vmem_limit_bytes=56 * 1024 * 1024
        ),
    )(tokens_t, routing, w_in, w_out)
    return out.T


def solution(mesh):
    in_specs = (P("seq", "exp"), P(None, "exp"), P("exp", None, "seq"), P("exp", "seq", None))
    out_specs = P("seq", "exp")
    step = functools.partial(shards, mesh.shape["exp"])
    return jax.shard_map(step, mesh=mesh, in_specs=in_specs, out_specs=out_specs, check_vma=False)
```

```python
import functools

import jax
import jax.numpy as jnp
from jax import lax
from jax.experimental import pallas as pl
from jax.experimental.pallas import tpu as pltpu
from jax.sharding import PartitionSpec as P

MESH = pl.DeviceIdType.MESH
F32, BF16 = jnp.float32, jnp.bfloat16
N = 4
CHIPS = N * N
ROWS = 64
HALF = ROWS // 2
TOK = 128
FSET = {1: (2, 1), -1: (-1, 0)}
FAR = [(2, 2), (2, 1), (2, 3), (1, 2), (3, 2), (1, 1), (3, 3), (1, 3), (3, 1), (2, 0), (0, 2), (1, 0), (3, 0), (0, 1), (0, 3)]


def spot(f):
    return f % N, (f // N - f % N) % N


def remote(src, dst, send, recv, seq, z):
    return pltpu.make_async_remote_copy(
        src_ref=src, dst_ref=dst, send_sem=send, recv_sem=recv, device_id=(seq, z), device_id_type=MESH
    )


def kernel(nz, tok_ref, route_ref, win_ref, wout_ref, out_ref, *scratch):
    (
        xt, gr, ge, lg, wt, cw, stok, s, rf, rn, rf2, rn2, fb, st, stp, facs, zs, zst, zb, si, sp, pacc,
        pt, pb, osend, orecv, oown, ofin, trow, trow_r, win, wout,
        tok_s, tok_r, xs_s, xs_r, rz_s, rz_r, ag_s, ag_r, ae_s, ae_r, rs_s, rs_r, st_s, st_r, zs_s, zs_r,
        zb_s, zb_r, si_s, si_r, pt_s, pt_r, ez_s, ez_r, os_s, os_r, fin_s, fin_r, tr_s, tr_r, w_s, own_s, own_o_s,
    ) = scratch
    seq, z = lax.axis_index("seq"), lax.axis_index("exp")
    x, y, c = seq // (2 * N), (seq // 2) % N, seq % 2
    p = seq // 2
    planes = nz // 2
    width = 128 * planes
    feats = xt.shape[0]
    fz = feats // nz
    owner = c == z % 2
    oc = z % 2
    mine = pl.multiple_of((z // 2) * 128, 128)
    other = 2 * p + 1 - c

    def zpeer(k):
        m = k // 2
        return (z + nz // 2 + m * (2 * (k % 2) - 1) + nz) % nz

    def owned(cx, cy):
        return N * ((cx + cy) % N) + cx

    def off_chip(dx, dy):
        return (x + dx) % N, (y + dy) % N

    def owned_by(q):
        return owned(q // N, q % N)

    mf = owned(x, y)

    def chip(k):
        return (p + k) % CHIPS

    def lanes(j):
        return pl.ds(pl.multiple_of(j * 128, 128), 128)

    def rows(i, n):
        return pl.ds(pl.multiple_of(i * n, n), n)

    def loop(lo, hi):
        def run(body):
            def step(i, carry):
                body(i)
                return carry
            lax.fori_loop(lo, hi, step, 0)
        return run

    ends = []

    def finish():
        for end in ends:
            end()

    barrier = pltpu.get_barrier_semaphore()

    @loop(1, nz)
    def _(k):
        pl.semaphore_signal(barrier, inc=1, device_id=(seq, zpeer(k)), device_id_type=MESH)

    @loop(1, CHIPS)
    def _(k):
        pl.semaphore_signal(barrier, inc=1, device_id=(2 * chip(k) + c, z), device_id_type=MESH)
        pl.semaphore_signal(barrier, inc=1, device_id=(2 * chip(k) + 1 - c, z), device_id_type=MESH)

    pl.semaphore_signal(barrier, inc=1, device_id=(other, z), device_id_type=MESH)

    own_x = pltpu.make_async_copy(tok_ref.at[:, lanes(z)], xt.at[rows(z, fz), lanes(c)], own_s.at[0])
    own_x.start()
    own_r = pltpu.make_async_copy(route_ref.at[rows(mf, ROWS), :], gr.at[x, y, :, pl.ds(mine, 128)], own_s.at[1])

    @pl.when(owner)
    def _():
        own_r.start()

    load_in = pltpu.make_async_copy(win_ref, win, w_s.at[0])
    load_out = pltpu.make_async_copy(wout_ref, wout, w_s.at[1])

    pl.semaphore_wait(barrier, nz - 1 + 2 * (CHIPS - 1) + 1)

    def rz_copy(k):
        return remote(
            route_ref.at[rows(mf, ROWS), :], gr.at[x, y, :, pl.ds(mine, 128)], rz_s.at[k], rz_r.at[z // 2], seq, zpeer(k)
        )

    @pl.when(owner)
    def _():
        @loop(1, nz)
        def _(k):
            rz_copy(k).start()

    def rz_end():
        @pl.when(owner)
        def _():
            @loop(1, nz)
            def _(k):
                rz_copy(k).wait_send()

    ends.append(rz_end)

    def tok_copy(k):
        to = zpeer(k)
        return remote(
            tok_ref.at[:, lanes(to)], xt.at[rows(z, fz), lanes(c)], tok_s.at[k], tok_r.at[z], seq, to
        )


    load_in.start()
    load_out.start()

    def near(h, axis, d):
        along_x = (axis == 1) == (h == 0)
        nx = (x + d) % N if along_x else x
        ny = y if along_x else (y + d) % N
        return 2 * (N * nx + ny) + c

    def place(h, o1, o2):
        return ((x + o1) % N, (y + o2) % N) if h == 0 else ((x + o2) % N, (y + o1) % N)

    def block(buf, h, o1, o2, lo=0, n=HALF):
        bx, by = place(h, o1, o2)
        return buf.at[bx, by, pl.ds(h * HALF + lo, n), :]

    OFF = (0, 1, -1, 2)
    QUART = HALF // 2

    def gather(buf, ss, rs, first=None, middle=None, second=None, third=None):
        def s1(h, d):
            b = block(buf, h, 0, 0)
            i = 16 * h + (0 if d == 1 else 1)
            return remote(b, b, ss.at[i], rs.at[i], near(h, 1, d), z)

        def s1f(h, d):
            b = block(buf, h, -d, 0, 0 if d == 1 else QUART, QUART)
            i = 16 * h + (2 if d == 1 else 3)
            return remote(b, b, ss.at[i], rs.at[i], near(h, 1, d), z)

        def s2(h, d, o):
            b = block(buf, h, o, 0)
            i = 16 * h + 4 + 4 * (d == -1) + OFF.index(o)
            return remote(b, b, ss.at[i], rs.at[i], near(h, 2, d), z)

        def s2f(h, d, o):
            b = block(buf, h, o, -d)
            i = 16 * h + 12 + 2 * (d == -1) + FSET[d].index(o)
            return remote(b, b, ss.at[i], rs.at[i], near(h, 2, d), z)

        both = (0, 1)
        dirs = (1, -1)

        def go(copy):
            copy.start()
            ends.append(copy.wait_send)

        def got1(h, d):
            b = block(buf, h, -d, 0)
            i = 16 * h + (0 if d == 1 else 1)
            remote(b, b, ss.at[i], rs.at[i], near(h, 1, d), z).wait_recv()

        def got1f(h, d):
            b = block(buf, h, 2, 0, 0 if d == 1 else QUART, QUART)
            i = 16 * h + (2 if d == 1 else 3)
            remote(b, b, ss.at[i], rs.at[i], near(h, 1, d), z).wait_recv()

        def got2(h, d, o):
            b = block(buf, h, o, -d)
            i = 16 * h + 4 + 4 * (d == -1) + OFF.index(o)
            remote(b, b, ss.at[i], rs.at[i], near(h, 2, d), z).wait_recv()

        def got2f(h, d, o):
            b = block(buf, h, o, 2)
            i = 16 * h + 12 + 2 * (d == -1) + FSET[d].index(o)
            remote(b, b, ss.at[i], rs.at[i], near(h, 2, d), z).wait_recv()

        for h in both:
            for d in dirs:
                go(s1(h, d))
        for h in both:
            for d in dirs:
                go(s2(h, d, 0))
        for d in dirs:
            for h in both:
                got1(h, d)
                go(s1f(h, d))
                go(s2(h, 1, -d))
                go(s2(h, -1, -d))
        for h in both:
            got2(h, -1, 0)
            go(s2f(h, -1, 0))
        for h in both:
            for d in dirs:
                got1f(h, d)
            for d in dirs:
                go(s2(h, d, 2))
        if first:
            first()
        for h in both:
            got2(h, 1, 1)
            go(s2f(h, 1, 1))
            got2(h, -1, -1)
            go(s2f(h, -1, -1))
        if middle:
            middle()
        for h in both:
            for d, o in ((1, 0), (1, -1), (-1, 1)):
                got2(h, d, o)
        if second:
            second()
        for h in both:
            got2(h, 1, 2)
            go(s2f(h, 1, 2))
        if third:
            third()
        for h in both:
            got2(h, -1, 2)
            for d in dirs:
                for o in FSET[d]:
                    got2f(h, d, o)

    def scatter(buf, ss, rs, started, summed):
        both = (0, 1)
        dirs = (1, -1)

        def go(copy):
            copy.start()
            ends.append(copy.wait_send)

        def slot_f(h, d, o):
            return 4 * h + 2 * (d == -1) + FSET[d].index(o)

        def slot_n(h, d, o):
            return 8 * h + 4 * (d == -1) + OFF.index(o)

        def slot_2(h, d):
            return 2 * h + (d == -1)

        def r1f(h, d, o):
            i = slot_f(h, d, o)
            return remote(block(buf, h, o, 2), rf.at[i], ss.at[i], rs.at[i], near(h, 2, d), z)

        def r1(h, d, o):
            i = slot_n(h, d, o)
            return remote(block(buf, h, o, d), rn.at[i], ss.at[8 + i], rs.at[8 + i], near(h, 2, d), z)

        def r2f(h, d):
            i = slot_2(h, d)
            b = block(buf, h, 2, 0, 0 if d == 1 else QUART, QUART)
            return remote(b, rf2.at[i], ss.at[24 + i], rs.at[24 + i], near(h, 1, d), z)

        def r2(h, d):
            i = slot_2(h, d)
            return remote(block(buf, h, d, 0), rn2.at[i], ss.at[28 + i], rs.at[28 + i], near(h, 1, d), z)

        for d, n in ((1, 0), (-1, 0), (1, 1), (-1, 1)):
            for h in both:
                go(r1f(h, d, FSET[d][n]))
        for h in both:
            go(r1(h, -1, 2))
            go(r1(h, 1, -1))
        for h in both:
            go(r1(h, -1, 1))
            go(r1(h, 1, 0))
        started()

        def scaled(val, i):
            return val.astype(F32) * facs[i : i + 1, :]

        def sender(h, d):
            return (3 if h == 0 else 1) + (d == 1)

        for d, n in ((1, 0), (-1, 0), (1, 1), (-1, 1)):
            for h in both:
                o = FSET[d][n]
                r1f(h, d, o).wait_recv()
                b = block(buf, h, o, d)
                b[...] = (scaled(b[...], 0) + scaled(rf[slot_f(h, d, o)], sender(h, d))).astype(BF16)
                go(r1(h, d, o))

        def total(h, o):
            val = scaled(block(buf, h, o, 0)[...], 0)
            for d in dirs:
                r1(h, d, o).wait_recv()
                part = rn[slot_n(h, d, o)]
                val += part.astype(F32) if o in FSET[d] else scaled(part, sender(h, d))
            return val

        for h in both:
            block(buf, h, 2, 0)[...] = total(h, 2).astype(BF16)
            go(r2f(h, 1))
            go(r2f(h, -1))
        summed()
        for h in both:
            for d in dirs:
                block(buf, h, d, 0)[...] = total(h, d).astype(BF16)
        for h in both:
            for d in dirs:
                r2f(h, d).wait_recv()
                b = block(buf, h, d, 0, 0 if d == 1 else QUART, QUART)
                b[...] = (b[...].astype(F32) + rf2[slot_2(h, d)].astype(F32)).astype(BF16)
                go(r2(h, d))
        for h in both:
            mid = total(h, 0)
            r2(h, 1).wait_recv()
            r2(h, -1).wait_recv()
            fb[pl.ds(h * HALF, HALF), :] = (
                mid + rn2[slot_2(h, 1)].astype(F32) + rn2[slot_2(h, -1)].astype(F32)
            ).astype(BF16)

    def from_planes(copy_of):
        @loop(0, planes)
        def _(j):
            @pl.when(2 * j + c != z)
            def _():
                copy_of(j).wait_recv()

    def rz_got(j):
        return remote(
            route_ref.at[rows(mf, ROWS), :], gr.at[x, y, :, lanes(j)], rz_s.at[0], rz_r.at[j], seq, z
        )

    from_planes(rz_got)

    @loop(1, nz)
    def _(k):
        tok_copy(k).start()

    def tok_end():
        @loop(1, nz)
        def _(k):
            tok_copy(k).wait_send()

    ends.append(tok_end)

    @pl.when(owner)
    def _():
        own_r.wait()

    groups = min(4, nz)
    per = nz // groups
    depth = feats // groups

    def xs_copy(g, half):
        b = xt.at[pl.ds(g * depth, depth), lanes(half)]
        return remote(b, b, xs_s.at[g], xs_r.at[g], other, z)

    def swap():
        for g in range(groups):
            for i in range(per):
                frm = g * per + i

                @pl.when(frm != z)
                def _():
                    remote(
                        tok_ref.at[:, lanes(z)], xt.at[pl.ds(frm * fz, fz), lanes(c)], tok_s.at[0], tok_r.at[frm], seq, z
                    ).wait_recv()

            xs_copy(g, c).start()
            ends.append(xs_copy(g, c).wait_send)

    own_x.wait()
    gather(gr, ag_s, ag_r, third=swap)
    for g in range(groups):
        xs_copy(g, 1 - c).wait_recv()

    stok[...] = xt[...].T
    tile = min(256, width)

    @loop(0, width // tile)
    def _(j):
        at = pl.ds(pl.multiple_of(j * tile, tile), tile)
        part = jnp.concatenate([gr[spot(f) + (slice(None), at)] for f in range(CHIPS)], axis=0)
        val = jnp.dot(stok[...], part, preferred_element_type=F32)
        lg[:, at] = val
        peak = jnp.max(val, axis=0, keepdims=True)
        expo = jnp.exp(val - peak)
        wt[:, at] = expo.astype(BF16)
        tot = jnp.sum(expo, axis=0, keepdims=True)
        for t in range(tile // 128):
            st[pl.ds(j * (tile // 128) + t, 1), :] = peak[:, 128 * t : 128 * (t + 1)]
            st[pl.ds(8 + j * (tile // 128) + t, 1), :] = tot[:, 128 * t : 128 * (t + 1)]

    if planes < 8:
        st[planes:8, :] = jnp.zeros((8 - planes, 128), F32)
        st[8 + planes : 16, :] = jnp.zeros((8 - planes, 128), F32)

    def st_copy(i):
        cx, cy = off_chip(*FAR[i])
        return remote(st, stp.at[p], st_s.at[i], st_r.at[p], 2 * (N * cx + cy) + c, z)

    for i in range(CHIPS - 1):
        st_copy(i).start()
        ends.append(st_copy(i).wait_send)
    stp[p] = st[...]

    for i in range(N):
        part = jnp.dot(xt[i * N * ROWS : (i + 1) * N * ROWS, :], wt[...], preferred_element_type=F32)
        for k in range(N):
            s[spot(N * i + k)] = part[k * ROWS : (k + 1) * ROWS, :].astype(BF16)

    def softmax():
        peak = jnp.max(lg[...], axis=1, keepdims=True)
        expo = jnp.exp(lg[...] - peak)
        cw[...] = expo.astype(BF16)
        tsum = jnp.sum(expo, axis=1, keepdims=True)
        peak_t = jnp.broadcast_to(peak, (2 * TOK, 128)).T
        tsum_t = jnp.broadcast_to(tsum, (2 * TOK, 128)).T
        trow[0:8, :] = peak_t[0:8, :]
        trow[8:16, :] = tsum_t[0:8, :]
        tr_copy.start()

    tr_copy = remote(trow, trow_r, tr_s.at[0], tr_r.at[0], other, z)
    ends.append(tr_copy.wait_send)

    def factors():
        @loop(1, CHIPS)
        def _(k):
            remote(st, stp.at[chip(k)], st_s.at[0], st_r.at[chip(k)], seq, z).wait_recv()

        high = jnp.max(stp[:, 0:8, :], axis=0)
        for i, (dx, dy) in enumerate(((0, 0), (1, 0), (-1, 0), (0, 1), (0, -1))):
            cx, cy = off_chip(dx, dy)
            fac = jnp.exp(stp[N * cx + cy, 0:8, :] - high)
            for j in range(planes):
                facs[i : i + 1, 128 * j : 128 * (j + 1)] = fac[j : j + 1, :]

    def totals():
        high = jnp.max(stp[:, 0:8, :], axis=0)
        tot = jnp.sum(jnp.exp(stp[:, 0:8, :] - high) * stp[:, 8:16, :], axis=0)
        for j in range(planes):
            zs[j, 0:1, :] = high[j : j + 1, :]
            zs[j, 1:2, :] = tot[j : j + 1, :]
            zs[j, 2:8, :] = jnp.zeros((6, 128), F32)
        to_planes(lambda j: zs_copy(j).start())

    def zs_copy(j):
        return remote(zs.at[j], zst.at[z], zs_s.at[j], zs_r.at[z], seq, 2 * j + c)

    def to_planes(do):
        @loop(1, nz)
        def _(k):
            to = zpeer(k)

            @pl.when(to % 2 == c)
            def _():
                do(to // 2)

    ends.append(lambda: to_planes(lambda j: zs_copy(j).wait_send()))

    def zs_got():
        @loop(1, nz)
        def _(k):
            frm = zpeer(k)
            remote(zs.at[0], zst.at[frm], zs_s.at[0], zs_r.at[frm], seq, z).wait_recv()

    scatter(s, rs_s, rs_r, factors, totals)

    def zb_copy(j):
        return remote(fb.at[:, lanes(j)], zb.at[z], zb_s.at[j], zb_r.at[z], seq, 2 * j + c)

    to_planes(lambda j: zb_copy(j).start())
    ends.append(lambda: to_planes(lambda j: zb_copy(j).wait_send()))
    softmax()

    def si_copy(dx, dy, core, sem):
        cx, cy = off_chip(dx, dy)
        return remote(si.at[mf], si.at[mf], sem, si_r.at[mf], 2 * (N * cx + cy) + core, z)

    si_all = [si_copy(dx, dy, core, si_s.at[2 * i + t]) for i, (dx, dy) in enumerate(FAR) for t, core in enumerate((c, 1 - c))]
    si_all.append(si_copy(0, 0, 1 - c, si_s.at[2 * CHIPS - 2]))

    @pl.when(owner)
    def _():
        zst[z] = zs[z // 2]
        zb[z] = fb[:, pl.ds(mine, 128)]

        zs_got()
        stat = zst[...]
        peaks = stat[:, 0:1, :]
        scale = jnp.exp(peaks - jnp.max(peaks, axis=0, keepdims=True))
        below = jnp.sum(scale * stat[:, 1:2, :], axis=0)

        @loop(1, nz)
        def _(k):
            frm = zpeer(k)
            remote(fb.at[:, lanes(0)], zb.at[frm], zb_s.at[0], zb_r.at[frm], seq, z).wait_recv()

        above = jnp.sum(scale * zb[...].astype(F32), axis=0)
        si[mf] = (above / below).astype(BF16)
        for copy in si_all:
            copy.start()

    def si_end():
        @pl.when(owner)
        def _():
            for copy in si_all:
                copy.wait_send()

    ends.append(si_end)

    @loop(1, CHIPS)
    def _(k):
        f = owned_by(chip(k))
        remote(si.at[f], si.at[f], si_s.at[0], si_r.at[f], seq, z).wait_recv()

    @pl.when(jnp.logical_not(owner))
    def _():
        remote(si.at[mf], si.at[mf], si_s.at[0], si_r.at[mf], seq, z).wait_recv()

    load_in.wait()
    load_out.wait()
    sp[...] = si[...].reshape(feats, 128).T
    experts = win.shape[0]
    each = 128 // experts

    @loop(0, experts)
    def _(e):
        h = jnp.dot(sp[rows(e, each), :], win[e], preferred_element_type=F32)
        h = jax.nn.gelu(h, approximate=True).astype(BF16)
        pacc[rows(e, each), :] = jnp.dot(h, wout[e], preferred_element_type=F32)

    pt[...] = pacc[...].T.astype(BF16).reshape(CHIPS, ROWS, 128)

    def pt_copy(dx, dy, i):
        cx, cy = off_chip(dx, dy)
        return remote(pt.at[owned(cx, cy)], pb.at[seq], pt_s.at[i], pt_r.at[seq], 2 * (N * cx + cy) + oc, z)

    for i, (dx, dy) in enumerate(FAR):
        pt_copy(dx, dy, i).start()
        ends.append(pt_copy(dx, dy, i).wait_send)
    pt_near = pt_copy(0, 0, CHIPS - 1)

    @pl.when(jnp.logical_not(owner))
    def _():
        pt_near.start()

    def pt_end():
        @pl.when(jnp.logical_not(owner))
        def _():
            pt_near.wait_send()

    ends.append(pt_end)

    def ez_copy(k):
        b = ge.at[x, y, :, pl.ds(mine, 128)]
        return remote(b, b, ez_s.at[k], ez_r.at[z // 2], seq, zpeer(k))

    @pl.when(owner)
    def _():
        pb[seq] = pt[mf]

        @loop(1, 2 * CHIPS)
        def _(k):
            frm = (seq + k) % (2 * CHIPS)
            remote(pt.at[0], pb.at[frm], pt_s.at[0], pt_r.at[frm], seq, z).wait_recv()

        ge[x, y, :, pl.ds(mine, 128)] = jnp.sum(pb[...].astype(F32), axis=0).astype(BF16)

        @loop(1, nz)
        def _(k):
            ez_copy(k).start()

    def ez_end():
        @pl.when(owner)
        def _():
            @loop(1, nz)
            def _(k):
                ez_copy(k).wait_send()

    ends.append(ez_end)

    def ez_got(j):
        b = ge.at[x, y, :, lanes(j)]
        return remote(b, b, ez_s.at[0], ez_r.at[j], seq, z)

    from_planes(ez_got)
    tr_copy.wait_recv()
    my = pl.multiple_of(c * TOK, TOK)
    peak_a, peak_b = trow[0:1, pl.ds(my, TOK)], trow_r[0:1, pl.ds(my, TOK)]
    sum_a, sum_b = trow[8:9, pl.ds(my, TOK)], trow_r[8:9, pl.ds(my, TOK)]
    top = jnp.maximum(peak_a, peak_b)
    fac_a, fac_b = jnp.exp(peak_a - top), jnp.exp(peak_b - top)
    under = fac_a * sum_a + fac_b * sum_b
    fac_a, fac_b = fac_a / under, fac_b / under

    pieces = [
        [(h, o1, 0) for h in (0, 1) for o1 in OFF],
        [(h, o1, o2) for h in (0, 1) for o1 in OFF[:3] for o2 in (1, -1)],
        [(h, o1, 2) for h in (0, 1) for o1 in OFF] + [(h, 2, o2) for h in (0, 1) for o2 in (1, -1)],
    ]
    starts = (0, 8, 20)
    each = CHIPS // nz

    def os_copy(g):
        part = pl.ds(starts[g], len(pieces[g]))
        return remote(osend.at[part], orecv.at[part], os_s.at[g], os_r.at[g], other, z)

    def mix(g):
        n = len(pieces[g])
        part = jnp.concatenate([block(ge, *piece)[...] for piece in pieces[g]], axis=0)
        val = lax.dot_general(part, cw[...], (((1,), (1,)), ((), ())), preferred_element_type=F32)
        first, second = val[:, :TOK], val[:, TOK:]
        at = pl.ds(starts[g], n)
        oown[at] = jnp.where(c == 0, first, second).reshape(n, HALF, TOK)
        osend[at] = jnp.where(c == 0, second, first).astype(BF16).reshape(n, HALF, TOK)
        os_copy(g).start()
        ends.append(os_copy(g).wait_send)

    def fin_copy(q, h, f):
        to = f // each
        at = out_ref.at[pl.ds(pl.multiple_of((f % each) * ROWS + h * HALF, HALF), HALF), lanes(z)]
        return remote(ofin.at[q], at, fin_s.at[q], fin_r.at[z, (f % each) * 2 + h], seq, to)

    def own_o(q, h, f):
        at = out_ref.at[pl.ds(pl.multiple_of((f % each) * ROWS + h * HALF, HALF), HALF), lanes(z)]
        return pltpu.make_async_copy(ofin.at[q], at, own_o_s.at[(f % each) * 2 + h])

    def send(g):
        os_copy(g).wait_recv()
        n = len(pieces[g])
        at = pl.ds(starts[g], n)
        ofin[at] = (oown[at] * fac_a + orecv[at].astype(F32) * fac_b).astype(BF16)
        for i, (h, o1, o2) in enumerate(pieces[g]):
            q = starts[g] + i
            f = owned(*place(h, o1, o2))

            @pl.when(f // each != z)
            def _():
                fin_copy(q, h, f).start()

            @pl.when(f // each == z)
            def _():
                own_o(q, h, f).start()

    gather(ge, ae_s, ae_r, first=lambda: mix(0), middle=lambda: send(0), second=lambda: mix(1), third=lambda: send(1))
    mix(2)
    send(2)

    @loop(0, 2 * each)
    def _(i):
        at = out_ref.at[pl.ds(pl.multiple_of(i * HALF, HALF), HALF), lanes(z)]
        pltpu.make_async_copy(ofin.at[0], at, own_o_s.at[i]).wait()

    @loop(1, nz)
    def _(k):
        frm = zpeer(k)
        for i in range(2 * each):
            at = out_ref.at[pl.ds(i * HALF, HALF), lanes(frm)]
            remote(ofin.at[0], at, fin_s.at[0], fin_r.at[frm, i], seq, z).wait_recv()

    for g in range(3):
        for i, (h, o1, o2) in enumerate(pieces[g]):
            f = owned(*place(h, o1, o2))

            @pl.when(f // each != z)
            def _():
                fin_copy(starts[g] + i, h, f).wait_send()

    finish()


def shards(nz, tokens, routing, w_in, w_out):
    tokens_t = tokens.T
    fz = tokens_t.shape[0]
    feats = fz * nz
    planes = nz // 2
    width = 128 * planes
    groups = min(4, nz)
    v, dma = pltpu.VMEM, pltpu.SemaphoreType.DMA
    scratch = [
        v((feats, 2 * TOK), BF16),
        v((N, N, ROWS, width), BF16),
        v((N, N, ROWS, width), BF16),
        v((2 * TOK, width), F32),
        v((2 * TOK, width), BF16),
        v((2 * TOK, width), BF16),
        v((2 * TOK, feats), BF16),
        v((N, N, ROWS, width), BF16),
        v((8, HALF, width), BF16),
        v((16, HALF, width), BF16),
        v((4, HALF // 2, width), BF16),
        v((4, HALF, width), BF16),
        v((ROWS, width), BF16),
        v((16, 128), F32),
        v((CHIPS, 16, 128), F32),
        v((8, width), F32),
        v((planes, 8, 128), F32),
        v((nz, 8, 128), F32),
        v((nz, ROWS, 128), BF16),
        v((CHIPS, ROWS, 128), BF16),
        v((128, feats), BF16),
        v((128, feats), F32),
        v((CHIPS, ROWS, 128), BF16),
        v((2 * CHIPS, ROWS, 128), BF16),
        v((2 * CHIPS, HALF, TOK), BF16),
        v((2 * CHIPS, HALF, TOK), BF16),
        v((2 * CHIPS, HALF, TOK), F32),
        v((2 * CHIPS, HALF, TOK), BF16),
        v((16, 2 * TOK), F32),
        v((16, 2 * TOK), F32),
        v(w_in.shape, BF16),
        v(w_out.shape, BF16),
    ]
    counts = [
        nz, nz, groups, groups, nz, planes, 32, 32, 32, 32, 32, 32, CHIPS, CHIPS, planes, nz,
        planes, nz, 2 * CHIPS, CHIPS, CHIPS, 2 * CHIPS, nz, planes, 3, 3, 2 * CHIPS, (nz, 2 * CHIPS // nz), 1, 1, 2, 3,
        2 * CHIPS // nz,
    ]
    scratch += [dma(n if isinstance(n, tuple) else (n,)) for n in counts]
    out = pl.pallas_call(
        functools.partial(kernel, nz),
        out_shape=jax.ShapeDtypeStruct(tokens_t.shape, BF16),
        in_specs=[pl.BlockSpec(memory_space=pl.ANY)] * 4,
        out_specs=pl.BlockSpec(memory_space=pl.ANY),
        scratch_shapes=scratch,
        compiler_params=pltpu.CompilerParams(
            collective_id=0, has_side_effects=True, vmem_limit_bytes=56 * 1024 * 1024
        ),
    )(tokens_t, routing, w_in, w_out)
    return out.T


def solution(mesh):
    in_specs = (P("seq", "exp"), P(None, "exp"), P("exp", None, "seq"), P("exp", "seq", None))
    out_specs = P("seq", "exp")
    step = functools.partial(shards, mesh.shape["exp"])
    return jax.shard_map(step, mesh=mesh, in_specs=in_specs, out_specs=out_specs, check_vma=False)
```

```python
import functools

import jax
import jax.numpy as jnp
from jax import lax
from jax.experimental import pallas as pl
from jax.experimental.pallas import tpu as pltpu
from jax.sharding import PartitionSpec as P

MESH = pl.DeviceIdType.MESH
F32, BF16 = jnp.float32, jnp.bfloat16
N = 4
CHIPS = N * N
ROWS = 64
HALF = ROWS // 2
TOK = 128
FSET = {1: (2, 1), -1: (-1, 0)}
FAR = [(2, 2), (2, 1), (2, 3), (1, 2), (3, 2), (1, 1), (3, 3), (1, 3), (3, 1), (2, 0), (0, 2), (1, 0), (3, 0), (0, 1), (0, 3)]


def spot(f):
    return f % N, (f // N - f % N) % N


def remote(src, dst, send, recv, seq, z):
    return pltpu.make_async_remote_copy(
        src_ref=src, dst_ref=dst, send_sem=send, recv_sem=recv, device_id=(seq, z), device_id_type=MESH
    )


def kernel(nz, tok_ref, route_ref, win_ref, wout_ref, out_ref, *scratch):
    (
        xt, gr, ge, lg, wt, cw, stok, s, rf, rn, rn2, fb, st, stp, facs, zs, zst, zb, si, sp, pacc,
        pt, pb, osend, orecv, oown, ofin, trow, trow_r, rv, tv, win, wout,
        tok_s, tok_r, xs_s, xs_r, rz_s, rz_r, ag_s, ag_r, ae_s, ae_r, rs_s, rs_r, st_s, st_r, zs_s, zs_r,
        zb_s, zb_r, si_s, si_r, pt_s, pt_r, ez_s, ez_r, os_s, os_r, fin_s, fin_r, tr_s, tr_r, w_s, own_s, own_o_s,
    ) = scratch
    seq, z = lax.axis_index("seq"), lax.axis_index("exp")
    x, y, c = seq // (2 * N), (seq // 2) % N, seq % 2
    p = seq // 2
    planes = nz // 2
    width = 128 * planes
    feats = xt.shape[0]
    fz = feats // nz
    owner = c == z % 2
    oc = z % 2
    mine = pl.multiple_of((z // 2) * 128, 128)
    other = 2 * p + 1 - c

    def zpeer(k):
        m = k // 2
        return (z + nz // 2 + m * (2 * (k % 2) - 1) + nz) % nz

    def owned(cx, cy):
        return N * ((cx + cy) % N) + cx

    def off_chip(dx, dy):
        return (x + dx) % N, (y + dy) % N

    def owned_by(q):
        return owned(q // N, q % N)

    mf = owned(x, y)

    def chip(k):
        return (p + k) % CHIPS

    def lanes(j):
        return pl.ds(pl.multiple_of(j * 128, 128), 128)

    def rows(i, n):
        return pl.ds(pl.multiple_of(i * n, n), n)

    def loop(lo, hi):
        def run(body):
            def step(i, carry):
                body(i)
                return carry
            lax.fori_loop(lo, hi, step, 0)
        return run

    ends = []

    def finish():
        for end in ends:
            end()

    barrier = pltpu.get_barrier_semaphore()

    @loop(1, nz)
    def _(k):
        pl.semaphore_signal(barrier, inc=1, device_id=(seq, zpeer(k)), device_id_type=MESH)

    @loop(1, CHIPS)
    def _(k):
        pl.semaphore_signal(barrier, inc=1, device_id=(2 * chip(k) + c, z), device_id_type=MESH)
        pl.semaphore_signal(barrier, inc=1, device_id=(2 * chip(k) + 1 - c, z), device_id_type=MESH)

    pl.semaphore_signal(barrier, inc=1, device_id=(other, z), device_id_type=MESH)

    own_r = pltpu.make_async_copy(route_ref.at[rows(mf, ROWS), :], gr.at[x, y, :, pl.ds(mine, 128)], own_s.at[1])

    @pl.when(owner)
    def _():
        own_r.start()

    load_in = pltpu.make_async_copy(win_ref, win, w_s.at[0])
    load_out = pltpu.make_async_copy(wout_ref, wout, w_s.at[1])
    stage_r = pltpu.make_async_copy(route_ref.at[rows(mf, ROWS), :], rv, own_s.at[2])
    stage_t = pltpu.make_async_copy(tok_ref, tv, own_s.at[0])
    stage_r.start()
    stage_t.start()
    load_in.start()
    load_out.start()
    stage_r.wait()
    stage_t.wait()
    xt[rows(z, fz), lanes(c)] = tv[:, lanes(z)]

    pl.semaphore_wait(barrier, nz - 1 + 2 * (CHIPS - 1) + 1)

    def rz_copy(k):
        return remote(
            rv, gr.at[x, y, :, pl.ds(mine, 128)], rz_s.at[k], rz_r.at[z // 2], seq, zpeer(k)
        )

    @pl.when(owner)
    def _():
        @loop(1, nz)
        def _(k):
            rz_copy(k).start()

    def rz_end():
        @pl.when(owner)
        def _():
            @loop(1, nz)
            def _(k):
                rz_copy(k).wait_send()

    ends.append(rz_end)

    def tok_copy(k):
        to = zpeer(k)
        return remote(
            tv.at[:, lanes(to)], xt.at[rows(z, fz), lanes(c)], tok_s.at[k], tok_r.at[z], seq, to
        )


    def near(h, axis, d):
        along_x = (axis == 1) == (h == 0)
        nx = (x + d) % N if along_x else x
        ny = y if along_x else (y + d) % N
        return 2 * (N * nx + ny) + c

    def place(h, o1, o2):
        return ((x + o1) % N, (y + o2) % N) if h == 0 else ((x + o2) % N, (y + o1) % N)

    def block(buf, h, o1, o2, lo=0, n=HALF):
        bx, by = place(h, o1, o2)
        return buf.at[bx, by, pl.ds(h * HALF + lo, n), :]

    OFF = (0, 1, -1, 2)
    ONE = (1, -1, 2)

    def gather(buf, ss, rs, first=None, middle=None, second=None, third=None, fourth=None):
        def s1(h, d):
            b = block(buf, h, 0, 0)
            i = 16 * h + ONE.index(d)
            return remote(b, b, ss.at[i], rs.at[i], near(h, 1, d), z)

        def s2(h, d, o):
            b = block(buf, h, o, 0)
            i = 16 * h + 4 + 4 * (d == -1) + OFF.index(o)
            return remote(b, b, ss.at[i], rs.at[i], near(h, 2, d), z)

        def s2f(h, d, o):
            b = block(buf, h, o, -d)
            i = 16 * h + 12 + 2 * (d == -1) + FSET[d].index(o)
            return remote(b, b, ss.at[i], rs.at[i], near(h, 2, d), z)

        both = (0, 1)
        dirs = (1, -1)

        def go(copy):
            copy.start()
            ends.append(copy.wait_send)

        def got1(h, d):
            b = block(buf, h, -d, 0)
            i = 16 * h + ONE.index(d)
            remote(b, b, ss.at[i], rs.at[i], near(h, 1, d), z).wait_recv()

        def got2(h, d, o):
            b = block(buf, h, o, -d)
            i = 16 * h + 4 + 4 * (d == -1) + OFF.index(o)
            remote(b, b, ss.at[i], rs.at[i], near(h, 2, d), z).wait_recv()

        def got2f(h, d, o):
            b = block(buf, h, o, 2)
            i = 16 * h + 12 + 2 * (d == -1) + FSET[d].index(o)
            remote(b, b, ss.at[i], rs.at[i], near(h, 2, d), z).wait_recv()

        for h in both:
            for d in (2, 1, -1):
                go(s1(h, d))
        for h in both:
            for d in dirs:
                go(s2(h, d, 0))
        for d in dirs:
            for h in both:
                got1(h, d)
                go(s2(h, 1, -d))
                go(s2(h, -1, -d))
        for h in both:
            got2(h, -1, 0)
            go(s2f(h, -1, 0))
        for h in both:
            got1(h, 2)
            for d in dirs:
                go(s2(h, d, 2))
        if first:
            first()
        for h in both:
            got2(h, 1, 1)
            go(s2f(h, 1, 1))
            got2(h, -1, -1)
            go(s2f(h, -1, -1))
        if middle:
            middle()
        for h in both:
            for d, o in ((1, 0), (1, -1), (-1, 1)):
                got2(h, d, o)
        if second:
            second()
        for h in both:
            got2(h, 1, 2)
            go(s2f(h, 1, 2))
        if third:
            third()
        for h in both:
            for d, o in ((1, 1), (-1, -1), (-1, 0)):
                got2f(h, d, o)
        if fourth:
            fourth()
        for h in both:
            got2(h, -1, 2)
            got2f(h, 1, 2)

    def scatter(buf, ss, rs, started, summed):
        both = (0, 1)
        dirs = (1, -1)

        def go(copy):
            copy.start()
            ends.append(copy.wait_send)

        def slot_f(h, d, o):
            return 4 * h + 2 * (d == -1) + FSET[d].index(o)

        def slot_n(h, d, o):
            return 8 * h + 4 * (d == -1) + OFF.index(o)

        def slot_2(h, d):
            return 3 * h + ONE.index(d)

        def r1f(h, d, o):
            i = slot_f(h, d, o)
            return remote(block(buf, h, o, 2), rf.at[i], ss.at[i], rs.at[i], near(h, 2, d), z)

        def r1(h, d, o):
            i = slot_n(h, d, o)
            return remote(block(buf, h, o, d), rn.at[i], ss.at[8 + i], rs.at[8 + i], near(h, 2, d), z)

        def r2(h, d):
            i = slot_2(h, d)
            return remote(block(buf, h, d, 0), rn2.at[i], ss.at[24 + i], rs.at[24 + i], near(h, 1, d), z)

        for d, n in ((1, 0), (-1, 0), (1, 1), (-1, 1)):
            for h in both:
                go(r1f(h, d, FSET[d][n]))
        for h in both:
            go(r1(h, -1, 2))
            go(r1(h, 1, -1))
        for h in both:
            go(r1(h, -1, 1))
            go(r1(h, 1, 0))
        started()

        def scaled(val, i):
            return val.astype(F32) * facs[i : i + 1, :]

        def sender(h, d):
            return (3 if h == 0 else 1) + (d == 1)

        for d, n in ((1, 0), (-1, 0), (1, 1), (-1, 1)):
            for h in both:
                o = FSET[d][n]
                r1f(h, d, o).wait_recv()
                b = block(buf, h, o, d)
                b[...] = (scaled(b[...], 0) + scaled(rf[slot_f(h, d, o)], sender(h, d))).astype(BF16)
                go(r1(h, d, o))

        def total(h, o):
            val = scaled(block(buf, h, o, 0)[...], 0)
            for d in dirs:
                r1(h, d, o).wait_recv()
                part = rn[slot_n(h, d, o)]
                val += part.astype(F32) if o in FSET[d] else scaled(part, sender(h, d))
            return val

        for h in both:
            block(buf, h, 2, 0)[...] = total(h, 2).astype(BF16)
            go(r2(h, 2))
        summed()
        for h in both:
            for d in dirs:
                block(buf, h, d, 0)[...] = total(h, d).astype(BF16)
                go(r2(h, d))
        for h in both:
            val = total(h, 0)
            for d in ONE:
                r2(h, d).wait_recv()
                val += rn2[slot_2(h, d)].astype(F32)
            fb[pl.ds(h * HALF, HALF), :] = val.astype(BF16)

    def from_planes(copy_of):
        @loop(0, planes)
        def _(j):
            @pl.when(2 * j + c != z)
            def _():
                copy_of(j).wait_recv()

    def rz_got(j):
        return remote(
            rv, gr.at[x, y, :, lanes(j)], rz_s.at[0], rz_r.at[j], seq, z
        )

    from_planes(rz_got)

    @loop(1, nz)
    def _(k):
        tok_copy(k).start()

    def tok_end():
        @loop(1, nz)
        def _(k):
            tok_copy(k).wait_send()

    ends.append(tok_end)

    @pl.when(owner)
    def _():
        own_r.wait()

    groups = min(4, nz)
    per = nz // groups
    depth = feats // groups

    def xs_copy(g, half):
        b = xt.at[pl.ds(g * depth, depth), lanes(half)]
        return remote(b, b, xs_s.at[g], xs_r.at[g], other, z)

    def swap():
        for g in range(groups):
            for i in range(per):
                frm = g * per + i

                @pl.when(frm != z)
                def _():
                    remote(
                        tv.at[:, lanes(z)], xt.at[pl.ds(frm * fz, fz), lanes(c)], tok_s.at[0], tok_r.at[frm], seq, z
                    ).wait_recv()

            xs_copy(g, c).start()
            ends.append(xs_copy(g, c).wait_send)

    gather(gr, ag_s, ag_r, third=swap)
    for g in range(groups):
        xs_copy(g, 1 - c).wait_recv()

    stok[...] = xt[...].T
    tile = min(256, width)

    @loop(0, width // tile)
    def _(j):
        at = pl.ds(pl.multiple_of(j * tile, tile), tile)
        part = jnp.concatenate([gr[spot(f) + (slice(None), at)] for f in range(CHIPS)], axis=0)
        val = jnp.dot(stok[...], part, preferred_element_type=F32)
        lg[:, at] = val
        peak = jnp.max(val, axis=0, keepdims=True)
        expo = jnp.exp(val - peak)
        wt[:, at] = expo.astype(BF16)
        tot = jnp.sum(expo, axis=0, keepdims=True)
        for t in range(tile // 128):
            st[pl.ds(j * (tile // 128) + t, 1), :] = peak[:, 128 * t : 128 * (t + 1)]
            st[pl.ds(8 + j * (tile // 128) + t, 1), :] = tot[:, 128 * t : 128 * (t + 1)]

    if planes < 8:
        st[planes:8, :] = jnp.zeros((8 - planes, 128), F32)
        st[8 + planes : 16, :] = jnp.zeros((8 - planes, 128), F32)

    def st_copy(i):
        cx, cy = off_chip(*FAR[i])
        return remote(st, stp.at[p], st_s.at[i], st_r.at[p], 2 * (N * cx + cy) + c, z)

    for i in range(CHIPS - 1):
        st_copy(i).start()
        ends.append(st_copy(i).wait_send)
    stp[p] = st[...]

    for i in range(N):
        part = jnp.dot(xt[i * N * ROWS : (i + 1) * N * ROWS, :], wt[...], preferred_element_type=F32)
        for k in range(N):
            s[spot(N * i + k)] = part[k * ROWS : (k + 1) * ROWS, :].astype(BF16)

    def softmax():
        peak = jnp.max(lg[...], axis=1, keepdims=True)
        expo = jnp.exp(lg[...] - peak)
        cw[...] = expo.astype(BF16)
        tsum = jnp.sum(expo, axis=1, keepdims=True)
        peak_t = jnp.broadcast_to(peak, (2 * TOK, 128)).T
        tsum_t = jnp.broadcast_to(tsum, (2 * TOK, 128)).T
        trow[0:8, :] = peak_t[0:8, :]
        trow[8:16, :] = tsum_t[0:8, :]
        tr_copy.start()

    tr_copy = remote(trow, trow_r, tr_s.at[0], tr_r.at[0], other, z)
    ends.append(tr_copy.wait_send)

    def factors():
        @loop(1, CHIPS)
        def _(k):
            remote(st, stp.at[chip(k)], st_s.at[0], st_r.at[chip(k)], seq, z).wait_recv()

        high = jnp.max(stp[:, 0:8, :], axis=0)
        for i, (dx, dy) in enumerate(((0, 0), (1, 0), (-1, 0), (0, 1), (0, -1))):
            cx, cy = off_chip(dx, dy)
            fac = jnp.exp(stp[N * cx + cy, 0:8, :] - high)
            for j in range(planes):
                facs[i : i + 1, 128 * j : 128 * (j + 1)] = fac[j : j + 1, :]

    def totals():
        high = jnp.max(stp[:, 0:8, :], axis=0)
        tot = jnp.sum(jnp.exp(stp[:, 0:8, :] - high) * stp[:, 8:16, :], axis=0)
        for j in range(planes):
            zs[j, 0:1, :] = high[j : j + 1, :]
            zs[j, 1:2, :] = tot[j : j + 1, :]
            zs[j, 2:8, :] = jnp.zeros((6, 128), F32)
        to_planes(lambda j: zs_copy(j).start())

    def zs_copy(j):
        return remote(zs.at[j], zst.at[z], zs_s.at[j], zs_r.at[z], seq, 2 * j + c)

    def to_planes(do):
        @loop(1, nz)
        def _(k):
            to = zpeer(k)

            @pl.when(to % 2 == c)
            def _():
                do(to // 2)

    ends.append(lambda: to_planes(lambda j: zs_copy(j).wait_send()))

    def zs_got():
        @loop(1, nz)
        def _(k):
            frm = zpeer(k)
            remote(zs.at[0], zst.at[frm], zs_s.at[0], zs_r.at[frm], seq, z).wait_recv()

    scatter(s, rs_s, rs_r, factors, totals)

    def zb_copy(j):
        return remote(fb.at[:, lanes(j)], zb.at[z], zb_s.at[j], zb_r.at[z], seq, 2 * j + c)

    to_planes(lambda j: zb_copy(j).start())
    ends.append(lambda: to_planes(lambda j: zb_copy(j).wait_send()))
    softmax()

    def si_copy(dx, dy, core, sem):
        cx, cy = off_chip(dx, dy)
        return remote(si.at[mf], si.at[mf], sem, si_r.at[mf], 2 * (N * cx + cy) + core, z)

    si_all = [si_copy(dx, dy, core, si_s.at[2 * i + t]) for i, (dx, dy) in enumerate(FAR) for t, core in enumerate((c, 1 - c))]
    si_all.append(si_copy(0, 0, 1 - c, si_s.at[2 * CHIPS - 2]))

    @pl.when(owner)
    def _():
        zst[z] = zs[z // 2]
        zb[z] = fb[:, pl.ds(mine, 128)]

        zs_got()
        stat = zst[...]
        peaks = stat[:, 0:1, :]
        scale = jnp.exp(peaks - jnp.max(peaks, axis=0, keepdims=True))
        below = jnp.sum(scale * stat[:, 1:2, :], axis=0)

        @loop(1, nz)
        def _(k):
            frm = zpeer(k)
            remote(fb.at[:, lanes(0)], zb.at[frm], zb_s.at[0], zb_r.at[frm], seq, z).wait_recv()

        above = jnp.sum(scale * zb[...].astype(F32), axis=0)
        si[mf] = (above / below).astype(BF16)
        for copy in si_all:
            copy.start()

    def si_end():
        @pl.when(owner)
        def _():
            for copy in si_all:
                copy.wait_send()

    ends.append(si_end)

    @loop(1, CHIPS)
    def _(k):
        f = owned_by(chip(k))
        remote(si.at[f], si.at[f], si_s.at[0], si_r.at[f], seq, z).wait_recv()

    @pl.when(jnp.logical_not(owner))
    def _():
        remote(si.at[mf], si.at[mf], si_s.at[0], si_r.at[mf], seq, z).wait_recv()

    load_in.wait()
    load_out.wait()
    sp[...] = si[...].reshape(feats, 128).T
    experts = win.shape[0]
    each = 128 // experts

    @loop(0, experts)
    def _(e):
        h = jnp.dot(sp[rows(e, each), :], win[e], preferred_element_type=F32)
        h = jax.nn.gelu(h, approximate=True).astype(BF16)
        pacc[rows(e, each), :] = jnp.dot(h, wout[e], preferred_element_type=F32)

    pt[...] = pacc[...].T.astype(BF16).reshape(CHIPS, ROWS, 128)

    def pt_copy(dx, dy, i):
        cx, cy = off_chip(dx, dy)
        return remote(pt.at[owned(cx, cy)], pb.at[seq], pt_s.at[i], pt_r.at[seq], 2 * (N * cx + cy) + oc, z)

    for i, (dx, dy) in enumerate(FAR):
        pt_copy(dx, dy, i).start()
        ends.append(pt_copy(dx, dy, i).wait_send)
    pt_near = pt_copy(0, 0, CHIPS - 1)

    @pl.when(jnp.logical_not(owner))
    def _():
        pt_near.start()

    def pt_end():
        @pl.when(jnp.logical_not(owner))
        def _():
            pt_near.wait_send()

    ends.append(pt_end)

    def ez_copy(k):
        b = ge.at[x, y, :, pl.ds(mine, 128)]
        return remote(b, b, ez_s.at[k], ez_r.at[z // 2], seq, zpeer(k))

    @pl.when(owner)
    def _():
        pb[seq] = pt[mf]

        @loop(1, 2 * CHIPS)
        def _(k):
            frm = (seq + k) % (2 * CHIPS)
            remote(pt.at[0], pb.at[frm], pt_s.at[0], pt_r.at[frm], seq, z).wait_recv()

        ge[x, y, :, pl.ds(mine, 128)] = jnp.sum(pb[...].astype(F32), axis=0).astype(BF16)

        @loop(1, nz)
        def _(k):
            ez_copy(k).start()

    def ez_end():
        @pl.when(owner)
        def _():
            @loop(1, nz)
            def _(k):
                ez_copy(k).wait_send()

    ends.append(ez_end)

    def ez_got(j):
        b = ge.at[x, y, :, lanes(j)]
        return remote(b, b, ez_s.at[0], ez_r.at[j], seq, z)

    from_planes(ez_got)
    tr_copy.wait_recv()
    my = pl.multiple_of(c * TOK, TOK)
    peak_a, peak_b = trow[0:1, pl.ds(my, TOK)], trow_r[0:1, pl.ds(my, TOK)]
    sum_a, sum_b = trow[8:9, pl.ds(my, TOK)], trow_r[8:9, pl.ds(my, TOK)]
    top = jnp.maximum(peak_a, peak_b)
    fac_a, fac_b = jnp.exp(peak_a - top), jnp.exp(peak_b - top)
    under = fac_a * sum_a + fac_b * sum_b
    fac_a, fac_b = fac_a / under, fac_b / under

    pieces = [
        [(h, o1, 0) for h in (0, 1) for o1 in OFF],
        [(h, o1, o2) for h in (0, 1) for o1 in OFF[:3] for o2 in (1, -1)],
        [(h, o1, 2) for h in (0, 1) for o1 in OFF[:3]],
        [(h, 2, o2) for h in (0, 1) for o2 in (1, -1, 2)],
    ]
    starts = (0, 8, 20, 26)
    each = CHIPS // nz

    def os_copy(g):
        part = pl.ds(starts[g], len(pieces[g]))
        return remote(osend.at[part], orecv.at[part], os_s.at[g], os_r.at[g], other, z)

    def mix(g):
        n = len(pieces[g])
        part = jnp.concatenate([block(ge, *piece)[...] for piece in pieces[g]], axis=0)
        val = lax.dot_general(part, cw[...], (((1,), (1,)), ((), ())), preferred_element_type=F32)
        first, second = val[:, :TOK], val[:, TOK:]
        at = pl.ds(starts[g], n)
        oown[at] = jnp.where(c == 0, first, second).reshape(n, HALF, TOK)
        osend[at] = jnp.where(c == 0, second, first).astype(BF16).reshape(n, HALF, TOK)
        os_copy(g).start()
        ends.append(os_copy(g).wait_send)

    def fin_copy(q, h, f):
        to = f // each
        at = out_ref.at[pl.ds(pl.multiple_of((f % each) * ROWS + h * HALF, HALF), HALF), lanes(z)]
        return remote(ofin.at[q], at, fin_s.at[q], fin_r.at[z, (f % each) * 2 + h], seq, to)

    def own_o(q, h, f):
        at = out_ref.at[pl.ds(pl.multiple_of((f % each) * ROWS + h * HALF, HALF), HALF), lanes(z)]
        return pltpu.make_async_copy(ofin.at[q], at, own_o_s.at[(f % each) * 2 + h])

    def send(g):
        os_copy(g).wait_recv()
        n = len(pieces[g])
        at = pl.ds(starts[g], n)
        ofin[at] = (oown[at] * fac_a + orecv[at].astype(F32) * fac_b).astype(BF16)
        for i, (h, o1, o2) in enumerate(pieces[g]):
            q = starts[g] + i
            f = owned(*place(h, o1, o2))

            @pl.when(f // each != z)
            def _():
                fin_copy(q, h, f).start()

            @pl.when(f // each == z)
            def _():
                own_o(q, h, f).start()

    gather(ge, ae_s, ae_r, first=lambda: mix(0), middle=lambda: send(0), second=lambda: mix(1), third=lambda: send(1), fourth=lambda: mix(2))
    mix(3)
    send(2)
    send(3)

    finish()
    @loop(0, 2 * each)
    def _(i):
        at = out_ref.at[pl.ds(pl.multiple_of(i * HALF, HALF), HALF), lanes(z)]
        pltpu.make_async_copy(ofin.at[0], at, own_o_s.at[i]).wait()

    @loop(1, nz)
    def _(k):
        frm = zpeer(k)
        for i in range(2 * each):
            at = out_ref.at[pl.ds(i * HALF, HALF), lanes(frm)]
            remote(ofin.at[0], at, fin_s.at[0], fin_r.at[frm, i], seq, z).wait_recv()

    for g in range(4):
        for i, (h, o1, o2) in enumerate(pieces[g]):
            f = owned(*place(h, o1, o2))

            @pl.when(f // each != z)
            def _():
                fin_copy(starts[g] + i, h, f).wait_send()


def shards(nz, tokens, routing, w_in, w_out):
    tokens_t = tokens.T
    fz = tokens_t.shape[0]
    feats = fz * nz
    planes = nz // 2
    width = 128 * planes
    groups = min(4, nz)
    v, dma = pltpu.VMEM, pltpu.SemaphoreType.DMA
    scratch = [
        v((feats, 2 * TOK), BF16),
        v((N, N, ROWS, width), BF16),
        v((N, N, ROWS, width), BF16),
        v((2 * TOK, width), F32),
        v((2 * TOK, width), BF16),
        v((2 * TOK, width), BF16),
        v((2 * TOK, feats), BF16),
        v((N, N, ROWS, width), BF16),
        v((8, HALF, width), BF16),
        v((16, HALF, width), BF16),
        v((6, HALF, width), BF16),
        v((ROWS, width), BF16),
        v((16, 128), F32),
        v((CHIPS, 16, 128), F32),
        v((8, width), F32),
        v((planes, 8, 128), F32),
        v((nz, 8, 128), F32),
        v((nz, ROWS, 128), BF16),
        v((CHIPS, ROWS, 128), BF16),
        v((128, feats), BF16),
        v((128, feats), F32),
        v((CHIPS, ROWS, 128), BF16),
        v((2 * CHIPS, ROWS, 128), BF16),
        v((2 * CHIPS, HALF, TOK), BF16),
        v((2 * CHIPS, HALF, TOK), BF16),
        v((2 * CHIPS, HALF, TOK), F32),
        v((2 * CHIPS, HALF, TOK), BF16),
        v((16, 2 * TOK), F32),
        v((16, 2 * TOK), F32),
        v((ROWS, 128), BF16),
        v(tokens_t.shape, BF16),
        v(w_in.shape, BF16),
        v(w_out.shape, BF16),
    ]
    counts = [
        nz, nz, groups, groups, nz, planes, 32, 32, 32, 32, 32, 32, CHIPS, CHIPS, planes, nz,
        planes, nz, 2 * CHIPS, CHIPS, CHIPS, 2 * CHIPS, nz, planes, 4, 4, 2 * CHIPS, (nz, 2 * CHIPS // nz), 1, 1, 2, 3,
        2 * CHIPS // nz,
    ]
    scratch += [dma(n if isinstance(n, tuple) else (n,)) for n in counts]
    out = pl.pallas_call(
        functools.partial(kernel, nz),
        out_shape=jax.ShapeDtypeStruct(tokens_t.shape, BF16),
        in_specs=[pl.BlockSpec(memory_space=pl.ANY)] * 4,
        out_specs=pl.BlockSpec(memory_space=pl.ANY),
        scratch_shapes=scratch,
        compiler_params=pltpu.CompilerParams(
            collective_id=0, has_side_effects=True, vmem_limit_bytes=56 * 1024 * 1024
        ),
    )(tokens_t, routing, w_in, w_out)
    return out.T


def solution(mesh):
    in_specs = (P("seq", "exp"), P(None, "exp"), P("exp", None, "seq"), P("exp", "seq", None))
    out_specs = P("seq", "exp")
    step = functools.partial(shards, mesh.shape["exp"])
    return jax.shard_map(step, mesh=mesh, in_specs=in_specs, out_specs=out_specs, check_vma=False)
```

```python
import functools

import jax
import jax.numpy as jnp
from jax import lax
from jax.experimental import pallas as pl
from jax.experimental.pallas import tpu as pltpu
from jax.sharding import PartitionSpec as P

MESH = pl.DeviceIdType.MESH
F32, BF16 = jnp.float32, jnp.bfloat16
N = 4
CHIPS = N * N
ROWS = 64
HALF = ROWS // 2
TOK = 128
FSET = {1: (2, 1), -1: (-1, 0)}
FAR = [(2, 2), (2, 1), (2, 3), (1, 2), (3, 2), (1, 1), (3, 3), (1, 3), (3, 1), (2, 0), (0, 2), (1, 0), (3, 0), (0, 1), (0, 3)]


def spot(f):
    return f % N, (f // N - f % N) % N


def remote(src, dst, send, recv, seq, z):
    return pltpu.make_async_remote_copy(
        src_ref=src, dst_ref=dst, send_sem=send, recv_sem=recv, device_id=(seq, z), device_id_type=MESH
    )


def kernel(nz, tok_ref, route_ref, win_ref, wout_ref, out_ref, *scratch):
    (
        xt, gr, ge, lg, wt, cw, stok, s, rf, rn, rn2, fb, st, stp, facs, zs, zst, zb, si, sp, pacc,
        pt, pb, osend, orecv, oown, ofin, trow, trow_r, rv, tv, win, wout,
        tok_s, tok_r, xs_s, xs_r, rz_s, rz_r, ag_s, ag_r, ae_s, ae_r, rs_s, rs_r, st_s, st_r, zs_s, zs_r,
        zb_s, zb_r, si_s, si_r, pt_s, pt_r, ez_s, ez_r, os_s, os_r, fin_s, fin_r, tr_s, tr_r, w_s, own_s, own_o_s,
    ) = scratch
    seq, z = lax.axis_index("seq"), lax.axis_index("exp")
    x, y, c = seq // (2 * N), (seq // 2) % N, seq % 2
    p = seq // 2
    planes = nz // 2
    width = 128 * planes
    feats = xt.shape[0]
    fz = feats // nz
    owner = c == z % 2
    oc = z % 2
    mine = pl.multiple_of((z // 2) * 128, 128)
    other = 2 * p + 1 - c

    def zpeer(k):
        m = k // 2
        return (z + nz // 2 + m * (2 * (k % 2) - 1) + nz) % nz

    def owned(cx, cy):
        return N * ((cx + cy) % N) + cx

    def off_chip(dx, dy):
        return (x + dx) % N, (y + dy) % N

    def owned_by(q):
        return owned(q // N, q % N)

    mf = owned(x, y)

    def chip(k):
        return (p + k) % CHIPS

    def lanes(j):
        return pl.ds(pl.multiple_of(j * 128, 128), 128)

    def rows(i, n):
        return pl.ds(pl.multiple_of(i * n, n), n)

    def loop(lo, hi):
        def run(body):
            def step(i, carry):
                body(i)
                return carry
            lax.fori_loop(lo, hi, step, 0)
        return run

    ends = []

    def finish():
        for end in ends:
            end()

    barrier = pltpu.get_barrier_semaphore()

    @loop(1, nz)
    def _(k):
        pl.semaphore_signal(barrier, inc=1, device_id=(seq, zpeer(k)), device_id_type=MESH)

    @loop(1, CHIPS)
    def _(k):
        pl.semaphore_signal(barrier, inc=1, device_id=(2 * chip(k) + c, z), device_id_type=MESH)
        pl.semaphore_signal(barrier, inc=1, device_id=(2 * chip(k) + 1 - c, z), device_id_type=MESH)

    pl.semaphore_signal(barrier, inc=1, device_id=(other, z), device_id_type=MESH)

    own_r = pltpu.make_async_copy(route_ref.at[rows(mf, ROWS), :], gr.at[x, y, :, pl.ds(mine, 128)], own_s.at[1])

    @pl.when(owner)
    def _():
        own_r.start()

    load_in = pltpu.make_async_copy(win_ref, win, w_s.at[0])
    load_out = pltpu.make_async_copy(wout_ref, wout, w_s.at[1])
    stage_r = pltpu.make_async_copy(route_ref.at[rows(mf, ROWS), :], rv, own_s.at[2])
    stage_t = pltpu.make_async_copy(tok_ref, tv, own_s.at[0])
    stage_r.start()
    stage_t.start()
    load_in.start()
    load_out.start()
    stage_r.wait()
    stage_t.wait()
    xt[rows(z, fz), lanes(c)] = tv[:, lanes(z)]

    pl.semaphore_wait(barrier, nz - 1 + 2 * (CHIPS - 1) + 1)

    def rz_copy(k):
        return remote(
            rv, gr.at[x, y, :, pl.ds(mine, 128)], rz_s.at[k], rz_r.at[z // 2], seq, zpeer(k)
        )

    @pl.when(owner)
    def _():
        @loop(1, nz)
        def _(k):
            rz_copy(k).start()

    def rz_end():
        @pl.when(owner)
        def _():
            @loop(1, nz)
            def _(k):
                rz_copy(k).wait_send()

    ends.append(rz_end)

    def tok_copy(k):
        to = zpeer(k)
        return remote(
            tv.at[:, lanes(to)], xt.at[rows(z, fz), lanes(c)], tok_s.at[k], tok_r.at[z], seq, to
        )


    def near(h, axis, d):
        along_x = (axis == 1) == (h == 0)
        nx = (x + d) % N if along_x else x
        ny = y if along_x else (y + d) % N
        return 2 * (N * nx + ny) + c

    def place(h, o1, o2):
        return ((x + o1) % N, (y + o2) % N) if h == 0 else ((x + o2) % N, (y + o1) % N)

    def block(buf, h, o1, o2, lo=0, n=HALF):
        bx, by = place(h, o1, o2)
        return buf.at[bx, by, pl.ds(h * HALF + lo, n), :]

    OFF = (0, 1, -1, 2)
    ONE = (1, -1, 2)

    def gather(buf, ss, rs, first=None, middle=None, second=None, third=None, fourth=None):
        def s1(h, d):
            b = block(buf, h, 0, 0)
            i = 16 * h + ONE.index(d)
            return remote(b, b, ss.at[i], rs.at[i], near(h, 1, d), z)

        def s2(h, d, o):
            b = block(buf, h, o, 0)
            i = 16 * h + 4 + 4 * (d == -1) + OFF.index(o)
            return remote(b, b, ss.at[i], rs.at[i], near(h, 2, d), z)

        def s2f(h, d, o):
            b = block(buf, h, o, -d)
            i = 16 * h + 12 + 2 * (d == -1) + FSET[d].index(o)
            return remote(b, b, ss.at[i], rs.at[i], near(h, 2, d), z)

        both = (0, 1)
        dirs = (1, -1)

        def go(copy):
            copy.start()
            ends.append(copy.wait_send)

        def got1(h, d):
            b = block(buf, h, -d, 0)
            i = 16 * h + ONE.index(d)
            remote(b, b, ss.at[i], rs.at[i], near(h, 1, d), z).wait_recv()

        def got2(h, d, o):
            b = block(buf, h, o, -d)
            i = 16 * h + 4 + 4 * (d == -1) + OFF.index(o)
            remote(b, b, ss.at[i], rs.at[i], near(h, 2, d), z).wait_recv()

        def got2f(h, d, o):
            b = block(buf, h, o, 2)
            i = 16 * h + 12 + 2 * (d == -1) + FSET[d].index(o)
            remote(b, b, ss.at[i], rs.at[i], near(h, 2, d), z).wait_recv()

        for h in both:
            for d in (2, 1, -1):
                go(s1(h, d))
        for h in both:
            for d in dirs:
                go(s2(h, d, 0))
        for d in dirs:
            for h in both:
                got1(h, d)
                go(s2(h, 1, -d))
                go(s2(h, -1, -d))
        for h in both:
            got2(h, -1, 0)
            go(s2f(h, -1, 0))
        for h in both:
            got1(h, 2)
            for d in dirs:
                go(s2(h, d, 2))
        if first:
            first()
        for h in both:
            got2(h, 1, 1)
            go(s2f(h, 1, 1))
            got2(h, -1, -1)
            go(s2f(h, -1, -1))
        if middle:
            middle()
        for h in both:
            for d, o in ((1, 0), (1, -1), (-1, 1)):
                got2(h, d, o)
        if second:
            second()
        for h in both:
            got2(h, 1, 2)
            go(s2f(h, 1, 2))
        if third:
            third()
        for h in both:
            for d, o in ((1, 1), (-1, -1), (-1, 0)):
                got2f(h, d, o)
        if fourth:
            fourth()
        for h in both:
            got2(h, -1, 2)
            got2f(h, 1, 2)

    def scatter(buf, ss, rs, started, summed):
        both = (0, 1)
        dirs = (1, -1)

        def go(copy):
            copy.start()
            ends.append(copy.wait_send)

        def slot_f(h, d, o):
            return 4 * h + 2 * (d == -1) + FSET[d].index(o)

        def slot_n(h, d, o):
            return 8 * h + 4 * (d == -1) + OFF.index(o)

        def slot_2(h, d):
            return 3 * h + ONE.index(d)

        def r1f(h, d, o):
            i = slot_f(h, d, o)
            return remote(block(buf, h, o, 2), rf.at[i], ss.at[i], rs.at[i], near(h, 2, d), z)

        def r1(h, d, o):
            i = slot_n(h, d, o)
            return remote(block(buf, h, o, d), rn.at[i], ss.at[8 + i], rs.at[8 + i], near(h, 2, d), z)

        def r2(h, d):
            i = slot_2(h, d)
            return remote(block(buf, h, d, 0), rn2.at[i], ss.at[24 + i], rs.at[24 + i], near(h, 1, d), z)

        for d, n in ((1, 0), (-1, 0), (1, 1), (-1, 1)):
            for h in both:
                go(r1f(h, d, FSET[d][n]))
        for h in both:
            go(r1(h, -1, 2))
            go(r1(h, 1, -1))
        for h in both:
            go(r1(h, -1, 1))
            go(r1(h, 1, 0))
        started()

        def scaled(val, i):
            return val.astype(F32) * facs[i : i + 1, :]

        def sender(h, d):
            return (3 if h == 0 else 1) + (d == 1)

        for d, n in ((1, 0), (-1, 0), (1, 1), (-1, 1)):
            for h in both:
                o = FSET[d][n]
                r1f(h, d, o).wait_recv()
                b = block(buf, h, o, d)
                b[...] = (scaled(b[...], 0) + scaled(rf[slot_f(h, d, o)], sender(h, d))).astype(BF16)
                go(r1(h, d, o))

        def total(h, o):
            val = scaled(block(buf, h, o, 0)[...], 0)
            for d in dirs:
                r1(h, d, o).wait_recv()
                part = rn[slot_n(h, d, o)]
                val += part.astype(F32) if o in FSET[d] else scaled(part, sender(h, d))
            return val

        for h in both:
            block(buf, h, 2, 0)[...] = total(h, 2).astype(BF16)
            go(r2(h, 2))
        summed()
        for h in both:
            for d in dirs:
                block(buf, h, d, 0)[...] = total(h, d).astype(BF16)
                go(r2(h, d))
        for h in both:
            val = total(h, 0)
            for d in ONE:
                r2(h, d).wait_recv()
                val += rn2[slot_2(h, d)].astype(F32)
            fb[pl.ds(h * HALF, HALF), :] = val.astype(BF16)

    def from_planes(copy_of):
        @loop(0, planes)
        def _(j):
            @pl.when(2 * j + c != z)
            def _():
                copy_of(j).wait_recv()

    def rz_got(j):
        return remote(
            rv, gr.at[x, y, :, lanes(j)], rz_s.at[0], rz_r.at[j], seq, z
        )

    @pl.when(owner)
    def _():
        @loop(1, nz)
        def _(k):
            tok_copy(k).start()

    from_planes(rz_got)

    @pl.when(jnp.logical_not(owner))
    def _():
        @loop(1, nz)
        def _(k):
            tok_copy(k).start()

    def tok_end():
        @loop(1, nz)
        def _(k):
            tok_copy(k).wait_send()

    ends.append(tok_end)

    @pl.when(owner)
    def _():
        own_r.wait()

    groups = min(4, nz)
    per = nz // groups
    depth = feats // groups

    def xs_copy(g, half):
        b = xt.at[pl.ds(g * depth, depth), lanes(half)]
        return remote(b, b, xs_s.at[g], xs_r.at[g], other, z)

    def swap():
        for g in range(groups):
            for i in range(per):
                frm = g * per + i

                @pl.when(frm != z)
                def _():
                    remote(
                        tv.at[:, lanes(z)], xt.at[pl.ds(frm * fz, fz), lanes(c)], tok_s.at[0], tok_r.at[frm], seq, z
                    ).wait_recv()

            xs_copy(g, c).start()
            ends.append(xs_copy(g, c).wait_send)

    gather(gr, ag_s, ag_r, third=swap)
    for g in range(groups):
        xs_copy(g, 1 - c).wait_recv()

    stok[...] = xt[...].T
    tile = min(256, width)

    @loop(0, width // tile)
    def _(j):
        at = pl.ds(pl.multiple_of(j * tile, tile), tile)
        part = jnp.concatenate([gr[spot(f) + (slice(None), at)] for f in range(CHIPS)], axis=0)
        val = jnp.dot(stok[...], part, preferred_element_type=F32)
        lg[:, at] = val
        peak = jnp.max(val, axis=0, keepdims=True)
        expo = jnp.exp(val - peak)
        wt[:, at] = expo.astype(BF16)
        tot = jnp.sum(expo, axis=0, keepdims=True)
        for t in range(tile // 128):
            st[pl.ds(j * (tile // 128) + t, 1), :] = peak[:, 128 * t : 128 * (t + 1)]
            st[pl.ds(8 + j * (tile // 128) + t, 1), :] = tot[:, 128 * t : 128 * (t + 1)]

    if planes < 8:
        st[planes:8, :] = jnp.zeros((8 - planes, 128), F32)
        st[8 + planes : 16, :] = jnp.zeros((8 - planes, 128), F32)

    def st_copy(i):
        cx, cy = off_chip(*FAR[i])
        return remote(st, stp.at[p], st_s.at[i], st_r.at[p], 2 * (N * cx + cy) + c, z)

    for i in range(CHIPS - 1):
        st_copy(i).start()
        ends.append(st_copy(i).wait_send)
    stp[p] = st[...]

    for i in range(N):
        part = jnp.dot(xt[i * N * ROWS : (i + 1) * N * ROWS, :], wt[...], preferred_element_type=F32)
        for k in range(N):
            s[spot(N * i + k)] = part[k * ROWS : (k + 1) * ROWS, :].astype(BF16)

    def softmax():
        peak = jnp.max(lg[...], axis=1, keepdims=True)
        expo = jnp.exp(lg[...] - peak)
        cw[...] = expo.astype(BF16)
        tsum = jnp.sum(expo, axis=1, keepdims=True)
        peak_t = jnp.broadcast_to(peak, (2 * TOK, 128)).T
        tsum_t = jnp.broadcast_to(tsum, (2 * TOK, 128)).T
        trow[0:8, :] = peak_t[0:8, :]
        trow[8:16, :] = tsum_t[0:8, :]
        tr_copy.start()

    tr_copy = remote(trow, trow_r, tr_s.at[0], tr_r.at[0], other, z)
    ends.append(tr_copy.wait_send)

    def factors():
        @loop(1, CHIPS)
        def _(k):
            remote(st, stp.at[chip(k)], st_s.at[0], st_r.at[chip(k)], seq, z).wait_recv()

        high = jnp.max(stp[:, 0:8, :], axis=0)
        for i, (dx, dy) in enumerate(((0, 0), (1, 0), (-1, 0), (0, 1), (0, -1))):
            cx, cy = off_chip(dx, dy)
            fac = jnp.exp(stp[N * cx + cy, 0:8, :] - high)
            for j in range(planes):
                facs[i : i + 1, 128 * j : 128 * (j + 1)] = fac[j : j + 1, :]

    def totals():
        high = jnp.max(stp[:, 0:8, :], axis=0)
        tot = jnp.sum(jnp.exp(stp[:, 0:8, :] - high) * stp[:, 8:16, :], axis=0)
        for j in range(planes):
            zs[j, 0:1, :] = high[j : j + 1, :]
            zs[j, 1:2, :] = tot[j : j + 1, :]
            zs[j, 2:8, :] = jnp.zeros((6, 128), F32)
        to_planes(lambda j: zs_copy(j).start())

    def zs_copy(j):
        return remote(zs.at[j], zst.at[z], zs_s.at[j], zs_r.at[z], seq, 2 * j + c)

    def to_planes(do):
        @loop(1, nz)
        def _(k):
            to = zpeer(k)

            @pl.when(to % 2 == c)
            def _():
                do(to // 2)

    ends.append(lambda: to_planes(lambda j: zs_copy(j).wait_send()))

    def zs_got():
        @loop(1, nz)
        def _(k):
            frm = zpeer(k)
            remote(zs.at[0], zst.at[frm], zs_s.at[0], zs_r.at[frm], seq, z).wait_recv()

    scatter(s, rs_s, rs_r, factors, totals)

    def zb_copy(j):
        return remote(fb.at[:, lanes(j)], zb.at[z], zb_s.at[j], zb_r.at[z], seq, 2 * j + c)

    to_planes(lambda j: zb_copy(j).start())
    ends.append(lambda: to_planes(lambda j: zb_copy(j).wait_send()))
    softmax()

    def si_copy(dx, dy, core, sem):
        cx, cy = off_chip(dx, dy)
        return remote(si.at[mf], si.at[mf], sem, si_r.at[mf], 2 * (N * cx + cy) + core, z)

    si_near = si_copy(0, 0, 1 - c, si_s.at[2 * CHIPS - 2])

    @pl.when(owner)
    def _():
        zst[z] = zs[z // 2]
        zb[z] = fb[:, pl.ds(mine, 128)]

        zs_got()
        stat = zst[...]
        peaks = stat[:, 0:1, :]
        scale = jnp.exp(peaks - jnp.max(peaks, axis=0, keepdims=True))
        below = jnp.sum(scale * stat[:, 1:2, :], axis=0)

        @loop(1, nz)
        def _(k):
            frm = zpeer(k)
            remote(fb.at[:, lanes(0)], zb.at[frm], zb_s.at[0], zb_r.at[frm], seq, z).wait_recv()

        above = jnp.sum(scale * zb[...].astype(F32), axis=0)
        si[mf] = (above / below).astype(BF16)
        si_near.start()

    @pl.when(jnp.logical_not(owner))
    def _():
        si_near.wait_recv()

    def si_end():
        @pl.when(owner)
        def _():
            si_near.wait_send()

    ends.append(si_end)

    for i, (dx, dy) in enumerate(FAR):
        si_copy(dx, dy, c, si_s.at[i]).start()
        ends.append(si_copy(dx, dy, c, si_s.at[i]).wait_send)

    @loop(1, CHIPS)
    def _(k):
        f = owned_by(chip(k))
        remote(si.at[f], si.at[f], si_s.at[0], si_r.at[f], seq, z).wait_recv()

    load_in.wait()
    load_out.wait()
    sp[...] = si[...].reshape(feats, 128).T
    experts = win.shape[0]
    each = 128 // experts

    @loop(0, experts)
    def _(e):
        h = jnp.dot(sp[rows(e, each), :], win[e], preferred_element_type=F32)
        h = jax.nn.gelu(h, approximate=True).astype(BF16)
        pacc[rows(e, each), :] = jnp.dot(h, wout[e], preferred_element_type=F32)

    pt[...] = pacc[...].T.astype(BF16).reshape(CHIPS, ROWS, 128)

    def pt_copy(dx, dy, i):
        cx, cy = off_chip(dx, dy)
        return remote(pt.at[owned(cx, cy)], pb.at[seq], pt_s.at[i], pt_r.at[seq], 2 * (N * cx + cy) + oc, z)

    for i, (dx, dy) in enumerate(FAR):
        pt_copy(dx, dy, i).start()
        ends.append(pt_copy(dx, dy, i).wait_send)
    pt_near = pt_copy(0, 0, CHIPS - 1)

    @pl.when(jnp.logical_not(owner))
    def _():
        pt_near.start()

    def pt_end():
        @pl.when(jnp.logical_not(owner))
        def _():
            pt_near.wait_send()

    ends.append(pt_end)

    def ez_copy(k):
        b = ge.at[x, y, :, pl.ds(mine, 128)]
        return remote(b, b, ez_s.at[k], ez_r.at[z // 2], seq, zpeer(k))

    @pl.when(owner)
    def _():
        pb[seq] = pt[mf]

        @loop(1, 2 * CHIPS)
        def _(k):
            frm = (seq + k) % (2 * CHIPS)
            remote(pt.at[0], pb.at[frm], pt_s.at[0], pt_r.at[frm], seq, z).wait_recv()

        ge[x, y, :, pl.ds(mine, 128)] = jnp.sum(pb[...].astype(F32), axis=0).astype(BF16)

        @loop(1, nz)
        def _(k):
            ez_copy(k).start()

    def ez_end():
        @pl.when(owner)
        def _():
            @loop(1, nz)
            def _(k):
                ez_copy(k).wait_send()

    ends.append(ez_end)

    def ez_got(j):
        b = ge.at[x, y, :, lanes(j)]
        return remote(b, b, ez_s.at[0], ez_r.at[j], seq, z)

    from_planes(ez_got)
    tr_copy.wait_recv()
    my = pl.multiple_of(c * TOK, TOK)
    peak_a, peak_b = trow[0:1, pl.ds(my, TOK)], trow_r[0:1, pl.ds(my, TOK)]
    sum_a, sum_b = trow[8:9, pl.ds(my, TOK)], trow_r[8:9, pl.ds(my, TOK)]
    top = jnp.maximum(peak_a, peak_b)
    fac_a, fac_b = jnp.exp(peak_a - top), jnp.exp(peak_b - top)
    under = fac_a * sum_a + fac_b * sum_b
    fac_a, fac_b = fac_a / under, fac_b / under

    pieces = [
        [(h, o1, 0) for h in (0, 1) for o1 in OFF],
        [(h, o1, o2) for h in (0, 1) for o1 in OFF[:3] for o2 in (1, -1)],
        [(h, o1, 2) for h in (0, 1) for o1 in OFF[:3]],
        [(h, 2, o2) for h in (0, 1) for o2 in (1, -1, 2)],
    ]
    starts = (0, 8, 20, 26)
    each = CHIPS // nz

    def os_copy(g):
        part = pl.ds(starts[g], len(pieces[g]))
        return remote(osend.at[part], orecv.at[part], os_s.at[g], os_r.at[g], other, z)

    def mix(g):
        n = len(pieces[g])
        part = jnp.concatenate([block(ge, *piece)[...] for piece in pieces[g]], axis=0)
        val = lax.dot_general(part, cw[...], (((1,), (1,)), ((), ())), preferred_element_type=F32)
        first, second = val[:, :TOK], val[:, TOK:]
        at = pl.ds(starts[g], n)
        oown[at] = jnp.where(c == 0, first, second).reshape(n, HALF, TOK)
        osend[at] = jnp.where(c == 0, second, first).astype(BF16).reshape(n, HALF, TOK)
        os_copy(g).start()
        ends.append(os_copy(g).wait_send)

    def fin_copy(q, h, f):
        to = f // each
        at = out_ref.at[pl.ds(pl.multiple_of((f % each) * ROWS + h * HALF, HALF), HALF), lanes(z)]
        return remote(ofin.at[q], at, fin_s.at[q], fin_r.at[z, (f % each) * 2 + h], seq, to)

    def own_o(q, h, f):
        at = out_ref.at[pl.ds(pl.multiple_of((f % each) * ROWS + h * HALF, HALF), HALF), lanes(z)]
        return pltpu.make_async_copy(ofin.at[q], at, own_o_s.at[(f % each) * 2 + h])

    def send(g):
        os_copy(g).wait_recv()
        n = len(pieces[g])
        at = pl.ds(starts[g], n)
        ofin[at] = (oown[at] * fac_a + orecv[at].astype(F32) * fac_b).astype(BF16)
        for i, (h, o1, o2) in enumerate(pieces[g]):
            q = starts[g] + i
            f = owned(*place(h, o1, o2))

            @pl.when(f // each != z)
            def _():
                fin_copy(q, h, f).start()

            @pl.when(f // each == z)
            def _():
                own_o(q, h, f).start()

    gather(ge, ae_s, ae_r, first=lambda: mix(0), middle=lambda: send(0), second=lambda: mix(1), third=lambda: send(1), fourth=lambda: mix(2))
    mix(3)
    send(2)
    send(3)

    finish()
    @loop(0, 2 * each)
    def _(i):
        at = out_ref.at[pl.ds(pl.multiple_of(i * HALF, HALF), HALF), lanes(z)]
        pltpu.make_async_copy(ofin.at[0], at, own_o_s.at[i]).wait()

    @loop(1, nz)
    def _(k):
        frm = zpeer(k)
        for i in range(2 * each):
            at = out_ref.at[pl.ds(i * HALF, HALF), lanes(frm)]
            remote(ofin.at[0], at, fin_s.at[0], fin_r.at[frm, i], seq, z).wait_recv()

    for g in range(4):
        for i, (h, o1, o2) in enumerate(pieces[g]):
            f = owned(*place(h, o1, o2))

            @pl.when(f // each != z)
            def _():
                fin_copy(starts[g] + i, h, f).wait_send()


def shards(nz, tokens, routing, w_in, w_out):
    tokens_t = tokens.T
    fz = tokens_t.shape[0]
    feats = fz * nz
    planes = nz // 2
    width = 128 * planes
    groups = min(4, nz)
    v, dma = pltpu.VMEM, pltpu.SemaphoreType.DMA
    scratch = [
        v((feats, 2 * TOK), BF16),
        v((N, N, ROWS, width), BF16),
        v((N, N, ROWS, width), BF16),
        v((2 * TOK, width), F32),
        v((2 * TOK, width), BF16),
        v((2 * TOK, width), BF16),
        v((2 * TOK, feats), BF16),
        v((N, N, ROWS, width), BF16),
        v((8, HALF, width), BF16),
        v((16, HALF, width), BF16),
        v((6, HALF, width), BF16),
        v((ROWS, width), BF16),
        v((16, 128), F32),
        v((CHIPS, 16, 128), F32),
        v((8, width), F32),
        v((planes, 8, 128), F32),
        v((nz, 8, 128), F32),
        v((nz, ROWS, 128), BF16),
        v((CHIPS, ROWS, 128), BF16),
        v((128, feats), BF16),
        v((128, feats), F32),
        v((CHIPS, ROWS, 128), BF16),
        v((2 * CHIPS, ROWS, 128), BF16),
        v((2 * CHIPS, HALF, TOK), BF16),
        v((2 * CHIPS, HALF, TOK), BF16),
        v((2 * CHIPS, HALF, TOK), F32),
        v((2 * CHIPS, HALF, TOK), BF16),
        v((16, 2 * TOK), F32),
        v((16, 2 * TOK), F32),
        v((ROWS, 128), BF16),
        v(tokens_t.shape, BF16),
        v(w_in.shape, BF16),
        v(w_out.shape, BF16),
    ]
    counts = [
        nz, nz, groups, groups, nz, planes, 32, 32, 32, 32, 32, 32, CHIPS, CHIPS, planes, nz,
        planes, nz, 2 * CHIPS, CHIPS, CHIPS, 2 * CHIPS, nz, planes, 4, 4, 2 * CHIPS, (nz, 2 * CHIPS // nz), 1, 1, 2, 3,
        2 * CHIPS // nz,
    ]
    scratch += [dma(n if isinstance(n, tuple) else (n,)) for n in counts]
    out = pl.pallas_call(
        functools.partial(kernel, nz),
        out_shape=jax.ShapeDtypeStruct(tokens_t.shape, BF16),
        in_specs=[pl.BlockSpec(memory_space=pl.ANY)] * 4,
        out_specs=pl.BlockSpec(memory_space=pl.ANY),
        scratch_shapes=scratch,
        compiler_params=pltpu.CompilerParams(
            collective_id=0, has_side_effects=True, vmem_limit_bytes=56 * 1024 * 1024
        ),
    )(tokens_t, routing, w_in, w_out)
    return out.T


def solution(mesh):
    in_specs = (P("seq", "exp"), P(None, "exp"), P("exp", None, "seq"), P("exp", "seq", None))
    out_specs = P("seq", "exp")
    step = functools.partial(shards, mesh.shape["exp"])
    return jax.shard_map(step, mesh=mesh, in_specs=in_specs, out_specs=out_specs, check_vma=False)
```

```python
import functools

import jax
import jax.numpy as jnp
from jax import lax
from jax.experimental import pallas as pl
from jax.experimental.pallas import tpu as pltpu
from jax.sharding import PartitionSpec as P

MESH = pl.DeviceIdType.MESH
F32, BF16 = jnp.float32, jnp.bfloat16
N = 4
CHIPS = N * N
ROWS = 64
HALF = ROWS // 2
TOK = 128
FSET = {1: (2, 1), -1: (-1, 0)}
FAR = [(2, 2), (2, 1), (2, 3), (1, 2), (3, 2), (1, 1), (3, 3), (1, 3), (3, 1), (2, 0), (0, 2), (1, 0), (3, 0), (0, 1), (0, 3)]


def spot(f):
    return f % N, (f // N - f % N) % N


def remote(src, dst, send, recv, seq, z):
    return pltpu.make_async_remote_copy(
        src_ref=src, dst_ref=dst, send_sem=send, recv_sem=recv, device_id=(seq, z), device_id_type=MESH
    )


def kernel(nz, tok_ref, route_ref, win_ref, wout_ref, out_ref, *scratch):
    (
        xt, gr, ge, lg, wt, cw, stok, s, rf, rn, rn2, fb, st, stp, facs, zs, zst, zb, si, sp, pacc,
        pt, pb, osend, orecv, oown, ofin, trow, trow_r, rv, tv, win, wout,
        tok_s, tok_r, xs_s, xs_r, rz_s, rz_r, ag_s, ag_r, ae_s, ae_r, rs_s, rs_r, st_s, st_r, zs_s, zs_r,
        zb_s, zb_r, si_s, si_r, pt_s, pt_r, ez_s, ez_r, os_s, os_r, fin_s, fin_r, tr_s, tr_r, w_s, own_s, own_o_s,
    ) = scratch
    seq, z = lax.axis_index("seq"), lax.axis_index("exp")
    x, y, c = seq // (2 * N), (seq // 2) % N, seq % 2
    p = seq // 2
    planes = nz // 2
    width = 128 * planes
    feats = xt.shape[0]
    fz = feats // nz
    owner = c == z % 2
    oc = z % 2
    mine = pl.multiple_of((z // 2) * 128, 128)
    other = 2 * p + 1 - c

    def zpeer(k):
        m = k // 2
        return (z + nz // 2 + m * (2 * (k % 2) - 1) + nz) % nz

    def owned(cx, cy):
        return N * ((cx + cy) % N) + cx

    def off_chip(dx, dy):
        return (x + dx) % N, (y + dy) % N

    def owned_by(q):
        return owned(q // N, q % N)

    mf = owned(x, y)

    def chip(k):
        return (p + k) % CHIPS

    def lanes(j):
        return pl.ds(pl.multiple_of(j * 128, 128), 128)

    def rows(i, n):
        return pl.ds(pl.multiple_of(i * n, n), n)

    def loop(lo, hi):
        def run(body):
            def step(i, carry):
                body(i)
                return carry
            lax.fori_loop(lo, hi, step, 0)
        return run

    ends = []

    def finish():
        for end in ends:
            end()

    barrier = pltpu.get_barrier_semaphore()

    @loop(1, nz)
    def _(k):
        pl.semaphore_signal(barrier, inc=1, device_id=(seq, zpeer(k)), device_id_type=MESH)

    @loop(1, CHIPS)
    def _(k):
        pl.semaphore_signal(barrier, inc=1, device_id=(2 * chip(k) + c, z), device_id_type=MESH)
        pl.semaphore_signal(barrier, inc=1, device_id=(2 * chip(k) + 1 - c, z), device_id_type=MESH)

    pl.semaphore_signal(barrier, inc=1, device_id=(other, z), device_id_type=MESH)

    own_r = pltpu.make_async_copy(route_ref.at[rows(mf, ROWS), :], gr.at[x, y, :, pl.ds(mine, 128)], own_s.at[1])

    @pl.when(owner)
    def _():
        own_r.start()

    load_in = pltpu.make_async_copy(win_ref, win, w_s.at[0])
    load_out = pltpu.make_async_copy(wout_ref, wout, w_s.at[1])
    stage_r = pltpu.make_async_copy(route_ref.at[rows(mf, ROWS), :], rv, own_s.at[2])
    stage_t = pltpu.make_async_copy(tok_ref, tv, own_s.at[0])
    stage_r.start()
    stage_t.start()
    load_in.start()
    load_out.start()
    stage_r.wait()
    stage_t.wait()
    xt[rows(z, fz), lanes(c)] = tv[:, lanes(z)]

    pl.semaphore_wait(barrier, nz - 1 + 2 * (CHIPS - 1) + 1)

    def rz_copy(k):
        return remote(
            rv, gr.at[x, y, :, pl.ds(mine, 128)], rz_s.at[k], rz_r.at[z // 2], seq, zpeer(k)
        )

    @pl.when(owner)
    def _():
        @loop(1, nz)
        def _(k):
            rz_copy(k).start()

    def rz_end():
        @pl.when(owner)
        def _():
            @loop(1, nz)
            def _(k):
                rz_copy(k).wait_send()

    ends.append(rz_end)

    def tok_copy(k):
        to = zpeer(k)
        return remote(
            tv.at[:, lanes(to)], xt.at[rows(z, fz), lanes(c)], tok_s.at[k], tok_r.at[z], seq, to
        )


    def near(h, axis, d):
        along_x = (axis == 1) == (h == 0)
        nx = (x + d) % N if along_x else x
        ny = y if along_x else (y + d) % N
        return 2 * (N * nx + ny) + c

    def place(h, o1, o2):
        return ((x + o1) % N, (y + o2) % N) if h == 0 else ((x + o2) % N, (y + o1) % N)

    def block(buf, h, o1, o2, lo=0, n=HALF):
        bx, by = place(h, o1, o2)
        return buf.at[bx, by, pl.ds(h * HALF + lo, n), :]

    OFF = (0, 1, -1, 2)
    ONE = (1, -1, 2)

    def gather(buf, ss, rs, first=None, middle=None, second=None, third=None, fourth=None):
        def s1(h, d):
            b = block(buf, h, 0, 0)
            i = 16 * h + ONE.index(d)
            return remote(b, b, ss.at[i], rs.at[i], near(h, 1, d), z)

        def s2(h, d, o):
            b = block(buf, h, o, 0)
            i = 16 * h + 4 + 4 * (d == -1) + OFF.index(o)
            return remote(b, b, ss.at[i], rs.at[i], near(h, 2, d), z)

        def s2f(h, d, o):
            b = block(buf, h, o, -d)
            i = 16 * h + 12 + 2 * (d == -1) + FSET[d].index(o)
            return remote(b, b, ss.at[i], rs.at[i], near(h, 2, d), z)

        both = (0, 1)
        dirs = (1, -1)

        def go(copy):
            copy.start()
            ends.append(copy.wait_send)

        def got1(h, d):
            b = block(buf, h, -d, 0)
            i = 16 * h + ONE.index(d)
            remote(b, b, ss.at[i], rs.at[i], near(h, 1, d), z).wait_recv()

        def got2(h, d, o):
            b = block(buf, h, o, -d)
            i = 16 * h + 4 + 4 * (d == -1) + OFF.index(o)
            remote(b, b, ss.at[i], rs.at[i], near(h, 2, d), z).wait_recv()

        def got2f(h, d, o):
            b = block(buf, h, o, 2)
            i = 16 * h + 12 + 2 * (d == -1) + FSET[d].index(o)
            remote(b, b, ss.at[i], rs.at[i], near(h, 2, d), z).wait_recv()

        for h in both:
            for d in (2, 1, -1):
                go(s1(h, d))
        for h in both:
            for d in dirs:
                go(s2(h, d, 0))
        for d in dirs:
            for h in both:
                got1(h, d)
                go(s2(h, 1, -d))
                go(s2(h, -1, -d))
        for h in both:
            got2(h, -1, 0)
            go(s2f(h, -1, 0))
        for h in both:
            got1(h, 2)
            for d in dirs:
                go(s2(h, d, 2))
        if first:
            first()
        for h in both:
            got2(h, 1, 1)
            go(s2f(h, 1, 1))
            got2(h, -1, -1)
            go(s2f(h, -1, -1))
        if middle:
            middle()
        for h in both:
            for d, o in ((1, 0), (1, -1), (-1, 1)):
                got2(h, d, o)
        if second:
            second()
        for h in both:
            got2(h, 1, 2)
            go(s2f(h, 1, 2))
        if third:
            third()
        for h in both:
            for d, o in ((1, 1), (-1, -1), (-1, 0)):
                got2f(h, d, o)
        if fourth:
            fourth()
        for h in both:
            got2(h, -1, 2)
            got2f(h, 1, 2)

    def scatter(buf, ss, rs, started, summed):
        both = (0, 1)
        dirs = (1, -1)

        def go(copy):
            copy.start()
            ends.append(copy.wait_send)

        def slot_f(h, d, o):
            return 4 * h + 2 * (d == -1) + FSET[d].index(o)

        def slot_n(h, d, o):
            return 8 * h + 4 * (d == -1) + OFF.index(o)

        def slot_2(h, d):
            return 3 * h + ONE.index(d)

        def r1f(h, d, o):
            i = slot_f(h, d, o)
            return remote(block(buf, h, o, 2), rf.at[i], ss.at[i], rs.at[i], near(h, 2, d), z)

        def r1(h, d, o):
            i = slot_n(h, d, o)
            return remote(block(buf, h, o, d), rn.at[i], ss.at[8 + i], rs.at[8 + i], near(h, 2, d), z)

        def r2(h, d):
            i = slot_2(h, d)
            return remote(block(buf, h, d, 0), rn2.at[i], ss.at[24 + i], rs.at[24 + i], near(h, 1, d), z)

        weighted(2)
        for d in dirs:
            for o in FSET[d]:
                go(r1f(1, d, o))
        go(r1f(0, 1, 2))
        weighted(1)
        go(r1f(0, 1, 1))
        weighted(-1)
        go(r1f(0, -1, -1))
        weighted(0)
        go(r1f(0, -1, 0))
        for h in both:
            go(r1(h, -1, 2))
            go(r1(h, 1, -1))
        for h in both:
            go(r1(h, -1, 1))
            go(r1(h, 1, 0))
        started()

        def scaled(val, i):
            return val.astype(F32) * facs[i : i + 1, :]

        def sender(h, d):
            return (3 if h == 0 else 1) + (d == 1)

        for d, n in ((1, 0), (-1, 0), (1, 1), (-1, 1)):
            for h in both:
                o = FSET[d][n]
                r1f(h, d, o).wait_recv()
                b = block(buf, h, o, d)
                b[...] = (scaled(b[...], 0) + scaled(rf[slot_f(h, d, o)], sender(h, d))).astype(BF16)
                go(r1(h, d, o))

        def total(h, o):
            val = scaled(block(buf, h, o, 0)[...], 0)
            for d in dirs:
                r1(h, d, o).wait_recv()
                part = rn[slot_n(h, d, o)]
                val += part.astype(F32) if o in FSET[d] else scaled(part, sender(h, d))
            return val

        for h in both:
            block(buf, h, 2, 0)[...] = total(h, 2).astype(BF16)
            go(r2(h, 2))
        summed()
        for h in both:
            for d in dirs:
                block(buf, h, d, 0)[...] = total(h, d).astype(BF16)
                go(r2(h, d))
        for h in both:
            val = total(h, 0)
            for d in ONE:
                r2(h, d).wait_recv()
                val += rn2[slot_2(h, d)].astype(F32)
            fb[pl.ds(h * HALF, HALF), :] = val.astype(BF16)

    def from_planes(copy_of):
        @loop(0, planes)
        def _(j):
            @pl.when(2 * j + c != z)
            def _():
                copy_of(j).wait_recv()

    def rz_got(j):
        return remote(
            rv, gr.at[x, y, :, lanes(j)], rz_s.at[0], rz_r.at[j], seq, z
        )

    @pl.when(owner)
    def _():
        @loop(1, nz)
        def _(k):
            tok_copy(k).start()

    from_planes(rz_got)

    @pl.when(jnp.logical_not(owner))
    def _():
        @loop(1, nz)
        def _(k):
            tok_copy(k).start()

    def tok_end():
        @loop(1, nz)
        def _(k):
            tok_copy(k).wait_send()

    ends.append(tok_end)

    @pl.when(owner)
    def _():
        own_r.wait()

    groups = min(4, nz)
    per = nz // groups
    depth = feats // groups

    def xs_copy(g, half):
        b = xt.at[pl.ds(g * depth, depth), lanes(half)]
        return remote(b, b, xs_s.at[g], xs_r.at[g], other, z)

    def swap():
        for g in range(groups):
            for i in range(per):
                frm = g * per + i

                @pl.when(frm != z)
                def _():
                    remote(
                        tv.at[:, lanes(z)], xt.at[pl.ds(frm * fz, fz), lanes(c)], tok_s.at[0], tok_r.at[frm], seq, z
                    ).wait_recv()

            xs_copy(g, c).start()
            ends.append(xs_copy(g, c).wait_send)

    gather(gr, ag_s, ag_r, third=swap)
    for g in range(groups):
        xs_copy(g, 1 - c).wait_recv()

    stok[...] = xt[...].T
    tile = min(256, width)

    @loop(0, width // tile)
    def _(j):
        at = pl.ds(pl.multiple_of(j * tile, tile), tile)
        part = jnp.concatenate([gr[spot(f) + (slice(None), at)] for f in range(CHIPS)], axis=0)
        val = jnp.dot(stok[...], part, preferred_element_type=F32)
        lg[:, at] = val
        peak = jnp.max(val, axis=0, keepdims=True)
        expo = jnp.exp(val - peak)
        wt[:, at] = expo.astype(BF16)
        tot = jnp.sum(expo, axis=0, keepdims=True)
        for t in range(tile // 128):
            st[pl.ds(j * (tile // 128) + t, 1), :] = peak[:, 128 * t : 128 * (t + 1)]
            st[pl.ds(8 + j * (tile // 128) + t, 1), :] = tot[:, 128 * t : 128 * (t + 1)]

    if planes < 8:
        st[planes:8, :] = jnp.zeros((8 - planes, 128), F32)
        st[8 + planes : 16, :] = jnp.zeros((8 - planes, 128), F32)

    def st_copy(i):
        cx, cy = off_chip(*FAR[i])
        return remote(st, stp.at[p], st_s.at[i], st_r.at[p], 2 * (N * cx + cy) + c, z)

    for i in range(CHIPS - 1):
        st_copy(i).start()
        ends.append(st_copy(i).wait_send)
    stp[p] = st[...]

    def weighted(o):
        bx = (x + o) % N
        part = jnp.concatenate([xt[rows(owned(bx, k), ROWS), :] for k in range(N)], axis=0)
        val = jnp.dot(part, wt[...], preferred_element_type=F32).astype(BF16)
        for k in range(N):
            s[bx, k] = val[k * ROWS : (k + 1) * ROWS, :]

    def softmax():
        peak = jnp.max(lg[...], axis=1, keepdims=True)
        expo = jnp.exp(lg[...] - peak)
        cw[...] = expo.astype(BF16)
        tsum = jnp.sum(expo, axis=1, keepdims=True)
        peak_t = jnp.broadcast_to(peak, (2 * TOK, 128)).T
        tsum_t = jnp.broadcast_to(tsum, (2 * TOK, 128)).T
        trow[0:8, :] = peak_t[0:8, :]
        trow[8:16, :] = tsum_t[0:8, :]
        tr_copy.start()

    tr_copy = remote(trow, trow_r, tr_s.at[0], tr_r.at[0], other, z)
    ends.append(tr_copy.wait_send)

    def factors():
        @loop(1, CHIPS)
        def _(k):
            remote(st, stp.at[chip(k)], st_s.at[0], st_r.at[chip(k)], seq, z).wait_recv()

        high = jnp.max(stp[:, 0:8, :], axis=0)
        for i, (dx, dy) in enumerate(((0, 0), (1, 0), (-1, 0), (0, 1), (0, -1))):
            cx, cy = off_chip(dx, dy)
            fac = jnp.exp(stp[N * cx + cy, 0:8, :] - high)
            for j in range(planes):
                facs[i : i + 1, 128 * j : 128 * (j + 1)] = fac[j : j + 1, :]

    def totals():
        high = jnp.max(stp[:, 0:8, :], axis=0)
        tot = jnp.sum(jnp.exp(stp[:, 0:8, :] - high) * stp[:, 8:16, :], axis=0)
        for j in range(planes):
            zs[j, 0:1, :] = high[j : j + 1, :]
            zs[j, 1:2, :] = tot[j : j + 1, :]
            zs[j, 2:8, :] = jnp.zeros((6, 128), F32)
        to_planes(lambda j: zs_copy(j).start())

    def zs_copy(j):
        return remote(zs.at[j], zst.at[z], zs_s.at[j], zs_r.at[z], seq, 2 * j + c)

    def to_planes(do):
        @loop(1, nz)
        def _(k):
            to = zpeer(k)

            @pl.when(to % 2 == c)
            def _():
                do(to // 2)

    ends.append(lambda: to_planes(lambda j: zs_copy(j).wait_send()))

    def zs_got():
        @loop(1, nz)
        def _(k):
            frm = zpeer(k)
            remote(zs.at[0], zst.at[frm], zs_s.at[0], zs_r.at[frm], seq, z).wait_recv()

    scatter(s, rs_s, rs_r, factors, totals)

    def zb_copy(j):
        return remote(fb.at[:, lanes(j)], zb.at[z], zb_s.at[j], zb_r.at[z], seq, 2 * j + c)

    to_planes(lambda j: zb_copy(j).start())
    ends.append(lambda: to_planes(lambda j: zb_copy(j).wait_send()))
    softmax()

    def si_copy(dx, dy, core, sem):
        cx, cy = off_chip(dx, dy)
        return remote(si.at[mf], si.at[mf], sem, si_r.at[mf], 2 * (N * cx + cy) + core, z)

    si_near = si_copy(0, 0, 1 - c, si_s.at[2 * CHIPS - 2])

    @pl.when(owner)
    def _():
        zst[z] = zs[z // 2]
        zb[z] = fb[:, pl.ds(mine, 128)]

        zs_got()
        stat = zst[...]
        peaks = stat[:, 0:1, :]
        scale = jnp.exp(peaks - jnp.max(peaks, axis=0, keepdims=True))
        below = jnp.sum(scale * stat[:, 1:2, :], axis=0)

        @loop(1, nz)
        def _(k):
            frm = zpeer(k)
            remote(fb.at[:, lanes(0)], zb.at[frm], zb_s.at[0], zb_r.at[frm], seq, z).wait_recv()

        above = jnp.sum(scale * zb[...].astype(F32), axis=0)
        si[mf] = (above / below).astype(BF16)
        si_near.start()

    @pl.when(jnp.logical_not(owner))
    def _():
        si_near.wait_recv()

    def si_end():
        @pl.when(owner)
        def _():
            si_near.wait_send()

    ends.append(si_end)

    for i, (dx, dy) in enumerate(FAR):
        si_copy(dx, dy, c, si_s.at[i]).start()
        ends.append(si_copy(dx, dy, c, si_s.at[i]).wait_send)

    @loop(1, CHIPS)
    def _(k):
        f = owned_by(chip(k))
        remote(si.at[f], si.at[f], si_s.at[0], si_r.at[f], seq, z).wait_recv()

    load_in.wait()
    load_out.wait()
    sp[...] = si[...].reshape(feats, 128).T
    experts = win.shape[0]
    each = 128 // experts

    @loop(0, experts)
    def _(e):
        h = jnp.dot(sp[rows(e, each), :], win[e], preferred_element_type=F32)
        h = jax.nn.gelu(h, approximate=True).astype(BF16)
        pacc[rows(e, each), :] = jnp.dot(h, wout[e], preferred_element_type=F32)

    pt[...] = pacc[...].T.astype(BF16).reshape(CHIPS, ROWS, 128)

    def pt_copy(dx, dy, i):
        cx, cy = off_chip(dx, dy)
        return remote(pt.at[owned(cx, cy)], pb.at[seq], pt_s.at[i], pt_r.at[seq], 2 * (N * cx + cy) + oc, z)

    for i, (dx, dy) in enumerate(FAR):
        pt_copy(dx, dy, i).start()
        ends.append(pt_copy(dx, dy, i).wait_send)
    pt_near = pt_copy(0, 0, CHIPS - 1)

    @pl.when(jnp.logical_not(owner))
    def _():
        pt_near.start()

    def pt_end():
        @pl.when(jnp.logical_not(owner))
        def _():
            pt_near.wait_send()

    ends.append(pt_end)

    def ez_copy(k):
        b = ge.at[x, y, :, pl.ds(mine, 128)]
        return remote(b, b, ez_s.at[k], ez_r.at[z // 2], seq, zpeer(k))

    @pl.when(owner)
    def _():
        pb[seq] = pt[mf]

        @loop(1, 2 * CHIPS)
        def _(k):
            frm = (seq + k) % (2 * CHIPS)
            remote(pt.at[0], pb.at[frm], pt_s.at[0], pt_r.at[frm], seq, z).wait_recv()

        ge[x, y, :, pl.ds(mine, 128)] = jnp.sum(pb[...].astype(F32), axis=0).astype(BF16)

        @loop(1, nz)
        def _(k):
            ez_copy(k).start()

    def ez_end():
        @pl.when(owner)
        def _():
            @loop(1, nz)
            def _(k):
                ez_copy(k).wait_send()

    ends.append(ez_end)

    def ez_got(j):
        b = ge.at[x, y, :, lanes(j)]
        return remote(b, b, ez_s.at[0], ez_r.at[j], seq, z)

    from_planes(ez_got)
    tr_copy.wait_recv()
    my = pl.multiple_of(c * TOK, TOK)
    peak_a, peak_b = trow[0:1, pl.ds(my, TOK)], trow_r[0:1, pl.ds(my, TOK)]
    sum_a, sum_b = trow[8:9, pl.ds(my, TOK)], trow_r[8:9, pl.ds(my, TOK)]
    top = jnp.maximum(peak_a, peak_b)
    fac_a, fac_b = jnp.exp(peak_a - top), jnp.exp(peak_b - top)
    under = fac_a * sum_a + fac_b * sum_b
    fac_a, fac_b = fac_a / under, fac_b / under

    pieces = [
        [(h, o1, 0) for h in (0, 1) for o1 in OFF],
        [(h, o1, o2) for h in (0, 1) for o1 in OFF[:3] for o2 in (1, -1)],
        [(h, o1, 2) for h in (0, 1) for o1 in OFF[:3]],
        [(h, 2, o2) for h in (0, 1) for o2 in (1, -1, 2)],
    ]
    starts = (0, 8, 20, 26)
    each = CHIPS // nz

    def os_copy(g):
        part = pl.ds(starts[g], len(pieces[g]))
        return remote(osend.at[part], orecv.at[part], os_s.at[g], os_r.at[g], other, z)

    def mix(g):
        n = len(pieces[g])
        part = jnp.concatenate([block(ge, *piece)[...] for piece in pieces[g]], axis=0)
        val = lax.dot_general(part, cw[...], (((1,), (1,)), ((), ())), preferred_element_type=F32)
        first, second = val[:, :TOK], val[:, TOK:]
        at = pl.ds(starts[g], n)
        oown[at] = jnp.where(c == 0, first, second).reshape(n, HALF, TOK)
        osend[at] = jnp.where(c == 0, second, first).astype(BF16).reshape(n, HALF, TOK)
        os_copy(g).start()
        ends.append(os_copy(g).wait_send)

    def fin_copy(q, h, f):
        to = f // each
        at = out_ref.at[pl.ds(pl.multiple_of((f % each) * ROWS + h * HALF, HALF), HALF), lanes(z)]
        return remote(ofin.at[q], at, fin_s.at[q], fin_r.at[z, (f % each) * 2 + h], seq, to)

    def own_o(q, h, f):
        at = out_ref.at[pl.ds(pl.multiple_of((f % each) * ROWS + h * HALF, HALF), HALF), lanes(z)]
        return pltpu.make_async_copy(ofin.at[q], at, own_o_s.at[(f % each) * 2 + h])

    def send(g):
        os_copy(g).wait_recv()
        n = len(pieces[g])
        at = pl.ds(starts[g], n)
        ofin[at] = (oown[at] * fac_a + orecv[at].astype(F32) * fac_b).astype(BF16)
        for i, (h, o1, o2) in enumerate(pieces[g]):
            q = starts[g] + i
            f = owned(*place(h, o1, o2))

            @pl.when(f // each != z)
            def _():
                fin_copy(q, h, f).start()

            @pl.when(f // each == z)
            def _():
                own_o(q, h, f).start()

    gather(ge, ae_s, ae_r, first=lambda: mix(0), middle=lambda: send(0), second=lambda: mix(1), third=lambda: send(1), fourth=lambda: mix(2))
    mix(3)
    send(2)
    send(3)

    finish()
    @loop(0, 2 * each)
    def _(i):
        at = out_ref.at[pl.ds(pl.multiple_of(i * HALF, HALF), HALF), lanes(z)]
        pltpu.make_async_copy(ofin.at[0], at, own_o_s.at[i]).wait()

    @loop(1, nz)
    def _(k):
        frm = zpeer(k)
        for i in range(2 * each):
            at = out_ref.at[pl.ds(i * HALF, HALF), lanes(frm)]
            remote(ofin.at[0], at, fin_s.at[0], fin_r.at[frm, i], seq, z).wait_recv()

    for g in range(4):
        for i, (h, o1, o2) in enumerate(pieces[g]):
            f = owned(*place(h, o1, o2))

            @pl.when(f // each != z)
            def _():
                fin_copy(starts[g] + i, h, f).wait_send()


def shards(nz, tokens, routing, w_in, w_out):
    tokens_t = tokens.T
    fz = tokens_t.shape[0]
    feats = fz * nz
    planes = nz // 2
    width = 128 * planes
    groups = min(4, nz)
    v, dma = pltpu.VMEM, pltpu.SemaphoreType.DMA
    scratch = [
        v((feats, 2 * TOK), BF16),
        v((N, N, ROWS, width), BF16),
        v((N, N, ROWS, width), BF16),
        v((2 * TOK, width), F32),
        v((2 * TOK, width), BF16),
        v((2 * TOK, width), BF16),
        v((2 * TOK, feats), BF16),
        v((N, N, ROWS, width), BF16),
        v((8, HALF, width), BF16),
        v((16, HALF, width), BF16),
        v((6, HALF, width), BF16),
        v((ROWS, width), BF16),
        v((16, 128), F32),
        v((CHIPS, 16, 128), F32),
        v((8, width), F32),
        v((planes, 8, 128), F32),
        v((nz, 8, 128), F32),
        v((nz, ROWS, 128), BF16),
        v((CHIPS, ROWS, 128), BF16),
        v((128, feats), BF16),
        v((128, feats), F32),
        v((CHIPS, ROWS, 128), BF16),
        v((2 * CHIPS, ROWS, 128), BF16),
        v((2 * CHIPS, HALF, TOK), BF16),
        v((2 * CHIPS, HALF, TOK), BF16),
        v((2 * CHIPS, HALF, TOK), F32),
        v((2 * CHIPS, HALF, TOK), BF16),
        v((16, 2 * TOK), F32),
        v((16, 2 * TOK), F32),
        v((ROWS, 128), BF16),
        v(tokens_t.shape, BF16),
        v(w_in.shape, BF16),
        v(w_out.shape, BF16),
    ]
    counts = [
        nz, nz, groups, groups, nz, planes, 32, 32, 32, 32, 32, 32, CHIPS, CHIPS, planes, nz,
        planes, nz, 2 * CHIPS, CHIPS, CHIPS, 2 * CHIPS, nz, planes, 4, 4, 2 * CHIPS, (nz, 2 * CHIPS // nz), 1, 1, 2, 3,
        2 * CHIPS // nz,
    ]
    scratch += [dma(n if isinstance(n, tuple) else (n,)) for n in counts]
    out = pl.pallas_call(
        functools.partial(kernel, nz),
        out_shape=jax.ShapeDtypeStruct(tokens_t.shape, BF16),
        in_specs=[pl.BlockSpec(memory_space=pl.ANY)] * 4,
        out_specs=pl.BlockSpec(memory_space=pl.ANY),
        scratch_shapes=scratch,
        compiler_params=pltpu.CompilerParams(
            collective_id=0, has_side_effects=True, vmem_limit_bytes=56 * 1024 * 1024
        ),
    )(tokens_t, routing, w_in, w_out)
    return out.T


def solution(mesh):
    in_specs = (P("seq", "exp"), P(None, "exp"), P("exp", None, "seq"), P("exp", "seq", None))
    out_specs = P("seq", "exp")
    step = functools.partial(shards, mesh.shape["exp"])
    return jax.shard_map(step, mesh=mesh, in_specs=in_specs, out_specs=out_specs, check_vma=False)
```
